512 devices in a mesh: grp: 8 (over y), ep: 64 (over x, z, core).
Axes of the slice: x: 4, y: 8, z: 8, core: 2. Of those that a mesh axis runs over, the one named last changes fastest.
Arguments:
- hidden_in: bfloat16 [4096, 2048], P('ep'), may hold values from -45 to 45
- query_nope: bfloat16 [4096, 2048], P('ep', 'grp'), may hold values from -6 to 6
- query_rope: bfloat16 [4096, 1024], P('ep', 'grp'), may hold values from -56 to 56
- new_latent: bfloat16 [1024, 2304], P('ep'), may hold values from -6 to 6
- latent_cache: bfloat16 [4096, 9216], P('ep'), may hold values from -6 to 6
- key_absorb: bfloat16 [16, 128, 512], P('grp'), may hold values from -0.5 to 0.5
- value_absorb: bfloat16 [16, 512, 128], P('grp'), may hold values from -1 to 1
- output_proj: bfloat16 [2048, 2048], P('grp'), may hold values from -0.125 to 0.125
- norm_gain: bfloat16 [2048], replicated, may hold values from 0.099609375 to 1.8984375
- router_proj: bfloat16 [2048, 64], replicated, may hold values from -0.125 to 0.125
- expert_ids: int32 [4096, 6], P('ep'), may hold values from 0 to 63, all different within a row; in each aligned block of 64 rows (0 to 63, 64 to 127, ...) at most 8 rows name the same one
- expert_gate: bfloat16 [64, 2048, 1408], P('ep', None, 'grp'), may hold values from -0.125 to 0.125
- expert_up: bfloat16 [64, 2048, 1408], P('ep', None, 'grp'), may hold values from -0.125 to 0.125
- expert_down: bfloat16 [64, 1408, 2048], P('ep', 'grp'), may hold values from -0.15625 to 0.15625
- block_table: int32 [1024, 64], P('ep'), may hold values from 0 to 191, as said below
- lengths: int32 [1024], P('ep'), may hold values from 1 to 1024
- subtree_moves: int32 [64, 64, 2], P('ep'), may hold values from -1 to 63, as said below
Outputs:
- mixed: bfloat16 [4096, 2048], P('ep', 'grp')
The draws below stay inside these ranges and needn't reach their ends.
Inputs may be any that keep to these rules, and one draw needn't show every extreme that they name: `expert_ids`: within the rows of one ep index no expert is named by more than 8 entries, a bound that some block reaches. `subtree_moves`: never the source itself; a live entry is a block id of the source; for every destination the rank after it sends 2 live blocks. `block_table`: an address names a resident block or a live moved block of that request's rank; the addresses of one request are distinct; the requests of a rank share a leading run of moved blocks.
All inputs are finite; a program needn't handle non-finite values.
Results may differ from the reference program's by a relative error of at most 0.0074.
Values may be sent and summed in bfloat16 or wider, within the bound.
A program may use at most 64 MiB of HBM per device.

```python
import math
import jax
import jax.numpy as jnp
import numpy as np
from jax import lax

D = 2048
H = 16
DN = 128
DR = 64
LAT = 512
DV = 128
FF = 1408
TOP = 6
STEPS = 4
BS = 16
MIG = 2
REQ = 16
TBL = 64
NB_RES = 64
EXPERTS = 64
REQS = 1024
ROWS = 4096
SLOTS_PER_RANK = 192
CAP = 8
N_EP = 64


def subtree_lists(key):
    key_live, key_blocks = jax.random.split(jax.random.fold_in(key, 101))
    live_slots = jax.random.randint(key_live, (N_EP, N_EP, MIG), 0, 2)
    ranks = jnp.arange(N_EP, dtype=jnp.int32)
    forced = (ranks[:, None] == (ranks[None, :] + 1) % N_EP)[:, :, None]
    diagonal = (ranks[:, None] == ranks[None, :])[:, :, None]
    live_slots = jnp.where(forced, 1, jnp.where(diagonal, 0, live_slots))
    block_ids = jax.random.randint(key_blocks, (N_EP, N_EP, MIG), 0, NB_RES)
    return jnp.where(live_slots == 1, block_ids, -1).astype(jnp.int32)


def order_slots(key, valid_mask, item_count):
    slot_addresses = jnp.arange(SLOTS_PER_RANK, dtype=jnp.int32)
    score_values = jax.random.randint(key, (item_count, SLOTS_PER_RANK), 0, 2 ** 20) * SLOTS_PER_RANK + slot_addresses[None, :]
    masked = jnp.where(valid_mask, score_values, -1)
    return jnp.argsort(-masked, axis=1).astype(jnp.int32)


def draw_subtree_moves(key, part):
    return subtree_lists(key)


def draw_block_table(key, part):
    moves = subtree_lists(key)
    key = jax.random.fold_in(key, 7)
    key_shared, key_own, key_span = jax.random.split(key, 3)
    incoming = jnp.transpose(moves >= 0, (1, 0, 2)).reshape(N_EP, N_EP * MIG)
    valid_in = jnp.concatenate([jnp.zeros((N_EP, NB_RES), bool), incoming], axis=1)
    valid_all = jnp.concatenate([jnp.ones((N_EP, NB_RES), bool), incoming], axis=1)
    shared_order = order_slots(key_shared, valid_in, N_EP)
    live_count = jnp.sum(incoming.astype(jnp.int32), axis=1)
    span = jnp.minimum(jax.random.randint(key_span, (N_EP,), TBL // 4, TBL // 2 + 1), live_count).astype(jnp.int32)
    rank_of_slot = jnp.argsort(shared_order, axis=1).astype(jnp.int32)
    in_shared = valid_in & (rank_of_slot < span[:, None])
    owner_rank = jnp.arange(REQS, dtype=jnp.int32) // REQ
    own_valid = valid_all[owner_rank] & jnp.logical_not(in_shared[owner_rank])
    own_order = order_slots(key_own, own_valid, REQS)
    position = jnp.arange(TBL, dtype=jnp.int32)
    request_span = span[owner_rank][:, None]
    from_shared = shared_order[owner_rank][:, :TBL]
    own_index = jnp.clip(position[None, :] - request_span, 0, TBL - 1).astype(jnp.int32)
    from_own = jnp.take_along_axis(own_order, own_index, axis=1)
    return jnp.where(position[None, :] < request_span, from_shared, from_own).astype(jnp.int32)


def draw_lengths(key, part):
    key = jax.random.fold_in(key, 11)
    sizes = jax.random.randint(key, (REQS,), 1, TBL * BS + 1)
    return sizes.at[0].set(TBL * BS).astype(jnp.int32)


def draw_new_latent(key, part):
    key = jax.random.fold_in(key, 3)
    values = jax.random.truncated_normal(key, -6.0, 6.0, (REQS, STEPS, LAT + DR), jnp.float32)
    return values.reshape(REQS, STEPS * (LAT + DR)).astype(jnp.bfloat16)


def draw_query_rope(key, part):
    key = jax.random.fold_in(key, 5)
    values = jax.random.truncated_normal(key, -6.0, 6.0, (REQS, STEPS, H, DR), jnp.float32)
    return values.reshape(REQS * STEPS, H * DR).astype(jnp.bfloat16)


def draw_hidden_in(key, part):
    key = jax.random.fold_in(key, 9)
    key_row, key_col, key_value = jax.random.split(key, 3)
    row_scale = jnp.exp(jax.random.uniform(key_row, (ROWS, 1), jnp.float32, math.log(0.3), math.log(3.0)))
    col_scale = jnp.exp(jax.random.uniform(key_col, (1, D), jnp.float32, math.log(0.3), math.log(3.0)))
    values = jax.random.truncated_normal(key_value, -4.0, 4.0, (ROWS, D), jnp.float32)
    return (values * row_scale * col_scale).astype(jnp.bfloat16)


def steps_of(own_key, shape, cuts, least, largest):
    gain = 1.0
    for dim, blocks in cuts:
        heights = jax.random.uniform(jax.random.fold_in(jax.random.fold_in(own_key, 6), dim), (blocks,), jnp.float32, least / len(cuts), largest / len(cuts))
        gain = gain * jnp.repeat(jnp.exp(heights), shape[dim] // blocks).reshape((-1,) + (1,) * (len(shape) - 1 - dim))
    return gain


def deal_out(rng, own, number, rows, amount, top, bound, slope):
    ranking = jax.random.permutation(rng, amount)
    crowded, usual = load_shares(amount, rows * top, bound, slope, True), load_shares(amount, rows * top, bound, slope, False)
    places = jnp.arange(amount)

    def named(sizes, rotation):
        used = int((sizes > 0).sum())
        fixed = max(1, used // 4)
        shifted = fixed + (places - fixed + rotation * (used - fixed)) % max(1, amount - fixed)
        return jnp.zeros((amount,), jnp.int32).at[ranking[jnp.where(places < fixed, places, shifted)]].set(jnp.asarray(sizes, jnp.int32))

    sizes = jnp.where(number % 4 == 0, named(crowded, number // 4), named(usual, number - number // 4 - 1))
    mixed = jax.random.permutation(jax.random.fold_in(own, 3), amount)
    source_of, sink = mixed[0:amount // 2 * 2:2], mixed[1:amount // 2 * 2:2]
    margin = jnp.minimum(sizes[source_of] - 1, bound - sizes[sink]) // 2
    margin = jnp.where((source_of == ranking[0]) | (sink == ranking[0]) | (sizes[sink] == 0), 0, jnp.maximum(margin, 0))
    shifted = jax.random.randint(jax.random.fold_in(own, 4), (amount // 2,), 0, 1 << 20) % (margin + 1)
    sizes = sizes.at[source_of].add(-shifted).at[sink].add(shifted)
    labels = jnp.searchsorted(jnp.cumsum(sizes), jnp.arange(rows * top), side="right").astype(jnp.int32)
    grid = labels.reshape(top, rows).T
    grid = grid[jax.random.permutation(jax.random.fold_in(own, 1), rows)]
    rotation = jax.random.randint(jax.random.fold_in(own, 2), (rows, 1), 0, top)
    return jnp.take_along_axis(grid, (jnp.arange(top)[None, :] + rotation) % top, axis=1)


def load_shares(amount, total, most, slope, full):
    loads = [(1 << 20) // math.isqrt(rank ** slope) + 1 for rank in range(1, amount + 1)]
    largest = most if full else min(most, max(-(-total // amount), total * loads[0] // sum(loads)))
    least = 1 if total - largest >= amount - 1 else 0
    given, spare = [largest] + [least] * (amount - 1), total - largest - least * (amount - 1)
    while spare > 0:
        free = [i for i in range(1, amount) if given[i] < largest] or [i for i in range(1, amount) if given[i] < most]
        pool, budget = sum([loads[i] for i in free]), spare
        for i in free:
            more = min(most - given[i], max(1, budget * loads[i] // pool), spare)
            given[i] = given[i] + more
            spare = spare - more
    return np.array(given)


def centred(rng, dims, spread, bound, cuts=(), held_as=jnp.bfloat16):
    array = jax.random.normal(rng, dims, jnp.float32) * spread
    if len(cuts) > 0:
        array = steps_of(rng, dims, cuts, -0.22, 0.18) * array
    return jnp.clip(array, min=-bound, max=bound).astype(held_as)


def setup_inputs(seed: int = 0) -> dict:
    splits = jax.random.split(jax.random.key(seed), 18)
    hidden_in = draw_hidden_in(jax.random.fold_in(splits[17], 71), 0)
    query_nope = centred(splits[1], (ROWS, H * DN), 1.0, 6.0, ((0, 64), (1, 8)))
    query_rope = draw_query_rope(jax.random.fold_in(splits[17], 71), 0)
    new_latent = draw_new_latent(jax.random.fold_in(splits[17], 71), 0)
    latent_cache = centred(splits[4], (N_EP * NB_RES, BS * (LAT + DR)), 1.0, 6.0, ((0, 64),))
    key_absorb = centred(splits[5], (H, DN, LAT), DN ** -0.5, 0.5, ((0, 8),))
    value_absorb = centred(splits[6], (H, LAT, DV), 32 ** -0.5, 1.0, ((0, 8),))
    output_proj = centred(splits[7], (H * DV, D), (H * DV) ** -0.5, 0.125, ((0, 8),))
    norm_gain = jnp.clip(1.0 + 0.18 * jax.random.normal(splits[8], (D,), jnp.float32), 0.099609375, 1.8984375).astype(jnp.bfloat16)
    router_proj = centred(splits[9], (D, EXPERTS), D ** -0.5, 0.125)
    expert_ids_keys = jax.random.split(jax.random.fold_in(splits[10], 1), ROWS // (REQ * STEPS))
    expert_ids_turns = jax.random.permutation(jax.random.fold_in(splits[10], 3), ROWS // (REQ * STEPS))
    expert_ids = jax.vmap(lambda own, number: deal_out(jax.random.fold_in(splits[10], 2), own, number, REQ * STEPS, EXPERTS, TOP, CAP, 2))(expert_ids_keys, expert_ids_turns).reshape((ROWS, TOP))
    expert_gate = centred(splits[11], (EXPERTS, D, FF), D ** -0.5, 0.125, ((0, 64), (2, 8)))
    expert_up = centred(splits[12], (EXPERTS, D, FF), D ** -0.5, 0.125, ((0, 64), (2, 8)))
    expert_down = centred(splits[13], (EXPERTS, FF, D), FF ** -0.5, 0.15625, ((0, 64), (1, 8)))
    block_table = draw_block_table(jax.random.fold_in(splits[17], 71), 0)
    lengths = draw_lengths(jax.random.fold_in(splits[17], 71), 0)
    subtree_moves = draw_subtree_moves(jax.random.fold_in(splits[17], 71), 0)
    return {"hidden_in": hidden_in, "query_nope": query_nope, "query_rope": query_rope, "new_latent": new_latent, "latent_cache": latent_cache, "key_absorb": key_absorb, "value_absorb": value_absorb, "output_proj": output_proj, "norm_gain": norm_gain, "router_proj": router_proj, "expert_ids": expert_ids, "expert_gate": expert_gate, "expert_up": expert_up, "expert_down": expert_down, "block_table": block_table, "lengths": lengths, "subtree_moves": subtree_moves}


def reference(hidden_in, query_nope, query_rope, new_latent, latent_cache, key_absorb, value_absorb, output_proj, norm_gain, router_proj, expert_ids, expert_gate, expert_up, expert_down, block_table, lengths, subtree_moves):
    key_width = LAT + DR
    scale_of_scores = (DN + DR) ** (-0.5)
    blocks = latent_cache.reshape(N_EP * NB_RES, BS, key_width)
    owner_rank = (jnp.arange(REQS, dtype=jnp.int32) // REQ)[:, None]
    offset = jnp.maximum(block_table - NB_RES, 0).astype(jnp.int32)
    source = offset // MIG
    within = offset % MIG
    moved_ids = subtree_moves[source, jnp.broadcast_to(owner_rank, source.shape), within]
    global_ids = jnp.where(block_table < NB_RES, owner_rank * NB_RES + block_table, source * NB_RES + moved_ids).astype(jnp.int32)
    q_latent = jnp.einsum('rhc,hcl->rhl', query_nope.reshape(ROWS, H, DN).astype(jnp.float32), key_absorb.astype(jnp.float32)).astype(jnp.bfloat16)
    queries = jnp.concatenate([q_latent, query_rope.reshape(ROWS, H, DR)], axis=2).reshape(REQS, STEPS * H, key_width)
    fresh_keys = new_latent.reshape(REQS, STEPS, key_width)
    cached = TBL * BS
    key_pos = jnp.arange(cached + STEPS, dtype=jnp.int32)
    row_step = jnp.arange(STEPS * H, dtype=jnp.int32) // H

    def attend(request):
        key_rows = jnp.concatenate([blocks[global_ids[request]].reshape(cached, key_width), fresh_keys[request]], axis=0)
        score_values = jnp.dot(queries[request], key_rows.T, preferred_element_type=jnp.float32) * scale_of_scores
        visible = jnp.where(key_pos[None, :] < cached, key_pos[None, :] < lengths[request], key_pos[None, :] - cached <= row_step[:, None])
        score_values = jnp.where(visible, score_values, -1e+30)
        row_peak = lax.optimization_barrier(jnp.max(score_values, axis=1, keepdims=True))
        exp_scores = jnp.exp(score_values - row_peak)
        attention = (exp_scores / lax.optimization_barrier(jnp.sum(exp_scores, axis=1, keepdims=True))).astype(jnp.bfloat16)
        return jnp.dot(attention, key_rows[:, :LAT], preferred_element_type=jnp.float32).astype(jnp.bfloat16)
    latent_out = lax.map(attend, jnp.arange(REQS, dtype=jnp.int32)).reshape(ROWS, H, LAT)
    head_out = jnp.einsum('rhl,hlv->rhv', latent_out.astype(jnp.float32), value_absorb.astype(jnp.float32)).astype(jnp.bfloat16).reshape(ROWS, H * DV)
    attention_out = jnp.dot(head_out, output_proj, preferred_element_type=jnp.float32)
    residual_state = hidden_in.astype(jnp.float32) + attention_out
    normed = (residual_state * lax.rsqrt(lax.optimization_barrier(jnp.mean(residual_state * residual_state, axis=1, keepdims=True)) + 1e-06) * norm_gain.astype(jnp.float32)).astype(jnp.bfloat16)
    logits = jnp.dot(normed, router_proj, preferred_element_type=jnp.float32)
    chosen = jax.nn.sigmoid(jnp.take_along_axis(logits, expert_ids, axis=1))
    gate_weights = chosen / lax.optimization_barrier(jnp.sum(chosen, axis=1, keepdims=True))
    flat_ids = expert_ids.reshape(N_EP, REQ * STEPS * TOP)
    onehot = (flat_ids[:, :, None] == jnp.arange(EXPERTS, dtype=jnp.int32)[None, None, :]).astype(jnp.int32)
    slot_index = lax.optimization_barrier(jnp.sum((jnp.cumsum(onehot, axis=1) - 1) * onehot, axis=2))
    target = (flat_ids * (N_EP * CAP) + jnp.arange(N_EP, dtype=jnp.int32)[:, None] * CAP + slot_index).reshape(ROWS * TOP).astype(jnp.int32)
    inputs = jnp.zeros((EXPERTS * N_EP * CAP, D), jnp.bfloat16).at[target].set(jnp.repeat(normed, TOP, axis=0))
    inputs = inputs.reshape(EXPERTS, N_EP * CAP, D)

    def expert_index(operands):
        expert_rows, gate_matrix, up_matrix, down_weight = operands
        gate_proj = jnp.dot(expert_rows, gate_matrix, preferred_element_type=jnp.float32)
        up_proj = jnp.dot(expert_rows, up_matrix, preferred_element_type=jnp.float32)
        activated = (jax.nn.silu(gate_proj) * up_proj).astype(jnp.bfloat16)
        return jnp.dot(activated, down_weight, preferred_element_type=jnp.float32)
    outputs = lax.map(expert_index, (inputs, expert_gate, expert_up, expert_down)).reshape(EXPERTS * N_EP * CAP, D)
    picked = outputs[target].reshape(ROWS, TOP, D)
    expert_mix = lax.optimization_barrier(jnp.sum(gate_weights[:, :, None] * picked, axis=1))
    return (residual_state + expert_mix).astype(jnp.bfloat16)
```

```python
import jax
import jax.numpy as jnp
from jax import lax
from jax.experimental import pallas as pl
from jax.experimental.pallas import tpu as pltpu
from jax.sharding import PartitionSpec as P

BF = jnp.bfloat16
F32 = jnp.float32
MESH = pl.DeviceIdType.MESH
NG = 8
NE = 64
NEG = -1e30


def iota(shape, dim):
    return lax.broadcasted_iota(jnp.int32, shape, dim)


def hot(condition):
    return jnp.where(condition, 1.0, 0.0).astype(BF)


def dot(a, b):
    return jnp.dot(a, b, preferred_element_type=F32)


def dot_nt(a, b):
    return lax.dot_general(a, b, (((1,), (1,)), ((), ())), preferred_element_type=F32)


def dot_tn(a, b):
    return lax.dot_general(a, b, (((0,), (0,)), ((), ())), preferred_element_type=F32)


def await_bytes(ref, sem):
    pltpu.make_async_copy(ref, ref, sem).wait()


def kernel(
    len_ref, hid, qn, qr, nl, ka, va, op, gain, router, ids, bt, mv, cache_hbm, wg_hbm, wu_hbm, wd_hbm,
    out,
    cache, wg, wu, wd, msg, pool, qe, qo, acc_e, acc_o, p3s, p3r, p4s, p4r, lgs, lgr, st, xs, gath,
    acc_g, acc_u, act, part, rsr, ys, ret,
    cache_sem, w_sem, e1s, e1r, a1s, a1r, p3ss, p3rs, p4ss, p4rs, lgss, lgrs, e2s, e2r, a2s, a2r, rss, rsrs, e3s, e3r,
):
    g = lax.axis_index("grp")
    me = lax.axis_index("ep")
    scale = (128 + 64) ** (-0.5)

    def peer(k):
        return lax.rem(g + (k + NG), NG)

    barrier = pltpu.get_barrier_semaphore()

    def greet(k, carry):
        pl.semaphore_signal(barrier, inc=1, device_id={"ep": lax.rem(me + k, NE)}, device_id_type=MESH)
        return carry

    lax.fori_loop(1, NE, greet, 0)
    for k in range(1, NG):
        pl.semaphore_signal(barrier, inc=1, device_id={"grp": peer(k)}, device_id_type=MESH)

    for p in range(8):
        pltpu.make_async_copy(cache_hbm.at[:, pl.ds(1152 * p, 1152)], cache.at[p], cache_sem).start()
    w_copies = [
        pltpu.make_async_copy(wg_hbm.at[0], wg, w_sem.at[0]),
        pltpu.make_async_copy(wu_hbm.at[0], wu, w_sem.at[1]),
        pltpu.make_async_copy(wd_hbm.at[0], wd, w_sem.at[2]),
    ]
    for copy in w_copies:
        copy.start()

    lo_me = lax.rem(me, 8)
    lo_to = lax.rem(g - lo_me + 8, 8)
    row = iota((128, 64), 0)
    sel = hot(iota((128, 64), 1) == lo_to + 8 * (row // 16))
    picked = dot(sel, mv[0].astype(F32).astype(BF))
    rk = iota((128, 1), 0)
    blk = jnp.where((rk // 8) % 2 == 0, picked[:, 0:1], picked[:, 1:2])
    code = jnp.where(blk < -0.5, -1.0, blk + (64 * (rk % 8)).astype(F32)).astype(jnp.int32)
    big = hot(iota((128, 512), 1) == code)
    await_bytes(cache, cache_sem)
    msg[...] = dot(big, cache[...].reshape(512, 1152)).astype(BF).reshape(8, 16, 1152)

    pl.semaphore_wait(barrier, NE - 1 + NG - 1)

    mine = me // 8
    for j in range(8):
        to = lo_to + 8 * j

        @pl.when(to == me)
        def _():
            pltpu.make_async_copy(msg.at[j], pool.at[g, mine], e1r.at[mine // 4]).start()

        @pl.when(to != me)
        def _():
            pltpu.make_async_remote_copy(
                msg.at[j], pool.at[g, mine], e1s, e1r.at[mine // 4], device_id={"ep": to}, device_id_type=MESH
            ).start()

    for h in range(2):
        rows = pl.ds(64 * h, 64)
        q_lat = dot(qn[:, 128 * h : 128 * h + 128], ka[h]).astype(BF)
        a, b = iota((128, 128), 0), iota((128, 128), 1)
        rope = dot(qr[...], hot((b < 64) & (a == b + 64 * h))).astype(BF)
        qe[rows, 0:512] = q_lat
        qe[rows, 512:640] = rope
    qo[...] = dot(qe[...], hot(iota((640, 640), 1) == iota((640, 640), 0) + 64)).astype(BF)

    req = iota((16, 64), 0)
    lens = jnp.zeros((16, 64), jnp.int32)
    for i in range(16):
        lens = jnp.where(req == i, len_ref[i], lens)
    count = jnp.clip(lens - 16 * iota((16, 64), 1), 0, 16)
    table = bt[...]
    addr = iota((16, 192), 1)
    usable = jnp.zeros((16, 192), jnp.int32)
    for p in range(64):
        usable = usable + jnp.where(table[:, p : p + 1] == addr, count[:, p : p + 1], 0)
    lam = iota((128, 16), 0)
    spread = hot((lam % 64) // 4 == iota((128, 16), 1))
    usable = dot(spread, usable.astype(F32).astype(BF)).astype(BF)

    acc_e[...] = jnp.zeros_like(acc_e)
    acc_o[...] = jnp.zeros_like(acc_o)

    def attend(x, c, m, l):
        even, odd = c > 0.5, c > 1.5
        s_e = jnp.where(even, dot_nt(qe[...], x[:, 0:640]) * scale, NEG)
        s_o = jnp.where(odd, dot_nt(qo[...], x[:, 512:1152]) * scale, NEG)
        peak = jnp.maximum(jnp.max(s_e, axis=1, keepdims=True), jnp.max(s_o, axis=1, keepdims=True))
        m_new = jnp.maximum(m, peak)
        p_e = jnp.where(even, jnp.exp(s_e - m_new), 0.0)
        p_o = jnp.where(odd, jnp.exp(s_o - m_new), 0.0)
        f = jnp.exp(m - m_new)
        l = l * f + jnp.sum(p_e, axis=1, keepdims=True) + jnp.sum(p_o, axis=1, keepdims=True)
        acc_e[...] = acc_e[...] * f + dot(p_e.astype(BF), x[:, 0:512])
        acc_o[...] = acc_o[...] * f + dot(p_o.astype(BF), x[:, 512:1152])
        return m_new, l

    stats = (jnp.full((128, 1), NEG, F32), jnp.zeros((128, 1), F32))
    lam, key = iota((128, 32), 0), iota((128, 32), 1)
    c_new = jnp.where((lam % 64) // 4 == key % 16, lam % 4 + 1 - 2 * (key // 16), 0).astype(F32)
    fresh = jnp.concatenate([nl[:, 0:1152], nl[:, 1152:2304]], axis=0)
    stats = attend(fresh, c_new, *stats)
    c_res = dot(usable, hot(iota((192, 128), 0) == iota((192, 128), 1) % 64))
    half_of = (iota((128, 128), 1) // 64).astype(F32)
    for q in range(4):
        x = cache[pl.ds(2 * q, 2)].reshape(128, 1152)
        stats = attend(x, c_res - 2.0 * (2 * q + half_of), *stats)

    def ring_gather(at, ssem, rsem, ready, on_chunk):
        def send(o, h, way):
            pltpu.make_async_remote_copy(
                at(o, h), at(o, h), ssem, rsem.at[h, o], device_id={"grp": peer(way)}, device_id_type=MESH
            ).start()

        def got(o, h):
            await_bytes(at(o, h), rsem.at[h, o])

        for h in range(2):
            ready(h)
            send(g, h, 1)
            send(g, h, -1)
        on_chunk(g)
        for t in range(3):
            a, b = peer(-1 - t), peer(1 + t)
            got(a, 0)
            send(a, 0, 1)
            got(b, 1)
            send(b, 1, -1)
            got(a, 1)
            if t < 2:
                send(a, 1, 1)
            got(b, 0)
            if t < 2:
                send(b, 0, -1)
            on_chunk(a)
            on_chunk(b)
        last = peer(4)
        got(last, 0)
        got(last, 1)
        on_chunk(last)

    carried = [stats]
    pair = ((iota((128, 128), 1) % 8) * 2).astype(F32)

    def attend_origin(o):
        col = iota((192, 128), 1)
        source = lax.rem(o - lo_me + 8, 8) + 8 * (col // 16)
        place = hot(iota((192, 128), 0) == 64 + 2 * source + (col // 8) % 2)
        c = dot(usable, place) - pair
        carried[0] = attend(pool[o].reshape(128, 1152), c, *carried[0])

    ring_gather(
        lambda o, h: pool.at[o, pl.ds(4 * h, 4)],
        a1s,
        a1r,
        lambda h: await_bytes(pool.at[g, pl.ds(4 * h, 4)], e1r.at[h]),
        attend_origin,
    )
    total = acc_e[...] + acc_o[...][:, 64:576]
    latent = (total / carried[0][1]).astype(BF)
    heads = [dot(latent[64 * h : 64 * h + 64], va[h]).astype(BF) for h in range(2)]
    term = dot(heads[0], op[0:128]) + dot(heads[1], op[128:256])
    for c in range(8):
        p3s[c] = term[:, 256 * c : 256 * c + 256].astype(BF)

    def exchange(src, dst, ssem, rsem):
        for k in range(1, NG):
            pltpu.make_async_remote_copy(
                src(peer(k)), dst.at[k - 1], ssem, rsem, device_id={"grp": peer(k)}, device_id_type=MESH
            ).start()

    exchange(lambda c: p3s.at[c], p3r, p3ss, p3rs)
    ids_v = ids[...]
    lane_e = iota((64, 64), 1)
    named = jnp.zeros((64, 64), F32)
    for k in range(6):
        named = named + jnp.where(ids_v[:, k : k + 1] == lane_e, 1.0, 0.0)
    named_b = named.astype(BF)
    before = dot(hot(iota((64, 64), 1) < iota((64, 64), 0)), named_b).astype(BF)
    widen = hot(iota((64, 512), 1) // 8 == iota((64, 512), 0))
    slot = (iota((64, 512), 1) % 8).astype(F32)
    chosen = (dot(named_b, widen) > 0.5) & (jnp.abs(dot(before, widen) - slot) < 0.5)
    chosen_b = hot(chosen)

    await_bytes(p3r, p3rs)
    cols = pl.ds(pl.multiple_of(g * 256, 256), 256)
    attn = p3s[g].astype(F32)
    for k in range(NG - 1):
        attn = attn + p3r[k].astype(F32)
    state = hid[:, cols].astype(F32) + attn
    st[...] = state
    square = jnp.sum(state * state, axis=1, keepdims=True)
    diagonal = iota((64, 128), 0) == iota((64, 128), 1)
    p4s[...] = jnp.broadcast_to(jnp.sum(jnp.where(diagonal, square, 0.0), axis=0, keepdims=True), (8, 128))
    exchange(lambda c: p4s, p4r, p4ss, p4rs)
    await_bytes(p4r, p4rs)
    squares = p4s[...]
    for k in range(NG - 1):
        squares = squares + p4r[k]
    square = jnp.sum(jnp.where(diagonal, squares[0:1], 0.0), axis=1, keepdims=True)
    inverse = lax.rsqrt(square / 2048.0 + 1e-06)
    normed = (state * inverse * gain[:, cols].astype(F32)).astype(BF)

    xs[...] = dot_tn(chosen_b, normed).reshape(64, 8, 256).astype(BF)
    pltpu.make_async_copy(xs.at[me], gath.at[g, me], e2r.at[me // 32]).start()

    def dispatch(k, carry):
        to = lax.rem(me + k, NE)
        pltpu.make_async_remote_copy(
            xs.at[to], gath.at[g, me], e2s, e2r.at[me // 32], device_id={"ep": to}, device_id_type=MESH
        ).start()
        return carry

    lax.fori_loop(1, NE, dispatch, 0)
    lgs[...] = dot(normed, router[pl.ds(pl.multiple_of(g * 256, 256), 256), :])
    exchange(lambda c: lgs, lgr, lgss, lgrs)
    for copy in w_copies:
        copy.wait()
    acc_g[...] = jnp.zeros_like(acc_g)
    acc_u[...] = jnp.zeros_like(acc_u)

    def expert_columns(o):
        x = gath[o].reshape(512, 256)
        rows = pl.ds(pl.multiple_of(o * 256, 256), 256)
        acc_g[...] += dot(x, wg[rows, :])
        acc_u[...] += dot(x, wu[rows, :])

    ring_gather(
        lambda o, h: gath.at[o, pl.ds(32 * h, 32)],
        a2s,
        a2r,
        lambda h: await_bytes(gath.at[g, pl.ds(32 * h, 32)], e2r.at[h]),
        expert_columns,
    )
    gate = acc_g[...]
    act[...] = (gate / (1.0 + jnp.exp(-gate)) * acc_u[...]).astype(BF)

    def make(c):
        lanes = pl.ds(pl.multiple_of(c * 256, 256), 256)
        part[c] = dot(act[...], wd[:, lanes]).reshape(64, 8, 256).astype(BF)

    def half(h):
        return pl.ds(32 * h, 32)

    def pass_on(c, h, way):
        d = 0 if way > 0 else 1
        pltpu.make_async_remote_copy(
            part.at[c, half(h)], rsr.at[d, c, half(h)], rss, rsrs.at[d, h, c],
            device_id={"grp": peer(way)}, device_id_type=MESH,
        ).start()

    def add_in(c, h, way):
        d = 0 if way > 0 else 1
        await_bytes(rsr.at[d, c, half(h)], rsrs.at[d, h, c])
        part[c, half(h)] = (part[c, half(h)].astype(F32) + rsr[d, c, half(h)].astype(F32)).astype(BF)

    make(peer(4))
    pass_on(peer(4), 0, 1)
    pass_on(peer(4), 1, -1)
    make(peer(3))
    pass_on(peer(3), 1, 1)
    make(peer(-3))
    pass_on(peer(-3), 0, -1)
    for t in range(1, 4):
        if t < 3:
            make(peer(3 - t))
            make(peer(t - 3))
        else:
            make(g)
        add_in(peer(4 - t), 0, 1)
        pass_on(peer(4 - t), 0, 1)
        add_in(peer(t - 4), 1, -1)
        pass_on(peer(t - 4), 1, -1)
        if t < 3:
            add_in(peer(3 - t), 1, 1)
            pass_on(peer(3 - t), 1, 1)
            add_in(peer(t - 3), 0, -1)
            pass_on(peer(t - 3), 0, -1)

    for h in range(2):
        total_h = part[g, half(h)].astype(F32)
        for d in range(2):
            await_bytes(rsr.at[d, g, half(h)], rsrs.at[d, h, g])
            total_h = total_h + rsr[d, g, half(h)].astype(F32)
        ys[half(h)] = total_h.astype(BF)

    pltpu.make_async_copy(ys.at[me], ret.at[me], e3r).start()

    def give_back(k, carry):
        to = lax.rem(me + k, NE)
        pltpu.make_async_remote_copy(
            ys.at[to], ret.at[me], e3s, e3r, device_id={"ep": to}, device_id_type=MESH
        ).start()
        return carry

    lax.fori_loop(1, NE, give_back, 0)

    await_bytes(lgr, lgrs)
    logits = lgs[...]
    for k in range(NG - 1):
        logits = logits + lgr[k]
    weight = jnp.where(named > 0.5, jax.nn.sigmoid(logits), 0.0)
    weight = weight / jnp.sum(weight, axis=1, keepdims=True)
    w_hi = weight.astype(BF)
    w_lo = (weight - w_hi.astype(F32)).astype(BF)
    mask = chosen_b.astype(F32)
    mix_hi = (dot(w_hi, widen) * mask).astype(BF)
    mix_lo = (dot(w_lo, widen) * mask).astype(BF)
    await_bytes(ret, e3r)
    results = ret[...].reshape(512, 256)
    out[...] = (st[...] + dot(mix_hi, results) + dot(mix_lo, results)).astype(BF)

    @pl.when(lax.rem(2 * me, 8) == g)
    def _():
        await_bytes(msg.at[pl.ds(0, 7)], e1s)

    @pl.when(lax.rem(2 * me, 8) != g)
    def _():
        await_bytes(msg, e1s)

    await_bytes(pool.at[pl.ds(0, 7)], a1s)
    await_bytes(p3s.at[pl.ds(0, 7)], p3ss)
    await_bytes(p4r, p4ss)
    await_bytes(lgr, lgss)
    await_bytes(xs.at[pl.ds(0, 63)], e2s)
    await_bytes(gath.at[pl.ds(0, 7)], a2s)
    await_bytes(part.at[pl.ds(0, 7)], rss)
    await_bytes(ys.at[pl.ds(0, 63)], e3s)


def local(
    hidden_in, query_nope, query_rope, new_latent, latent_cache, key_absorb, value_absorb, output_proj, norm_gain,
    router_proj, expert_ids, expert_gate, expert_up, expert_down, block_table, lengths, subtree_moves,
):
    vmem = pl.BlockSpec(memory_space=pltpu.VMEM)
    anywhere = pl.BlockSpec(memory_space=pl.ANY)
    dma = pltpu.SemaphoreType.DMA
    v = pltpu.VMEM
    return pl.pallas_call(
        kernel,
        out_shape=jax.ShapeDtypeStruct((64, 256), BF),
        in_specs=[pl.BlockSpec(memory_space=pltpu.SMEM)] + [vmem] * 12 + [anywhere] * 4,
        out_specs=vmem,
        scratch_shapes=[
            v((8, 64, 1152), BF),
            v((2048, 176), BF),
            v((2048, 176), BF),
            v((176, 2048), BF),
            v((8, 16, 1152), BF),
            v((8, 8, 16, 1152), BF),
            v((128, 640), BF),
            v((128, 640), BF),
            v((128, 512), F32),
            v((128, 640), F32),
            v((8, 64, 256), BF),
            v((7, 64, 256), BF),
            v((8, 128), F32),
            v((7, 8, 128), F32),
            v((64, 64), F32),
            v((7, 64, 64), F32),
            v((64, 256), F32),
            v((64, 8, 256), BF),
            v((8, 64, 8, 256), BF),
            v((512, 176), F32),
            v((512, 176), F32),
            v((512, 176), BF),
            v((8, 64, 8, 256), BF),
            v((2, 8, 64, 8, 256), BF),
            v((64, 8, 256), BF),
            v((64, 8, 256), BF),
            dma, dma((3,)),
            dma, dma((2,)), dma, dma((2, 8)),
            dma, dma, dma, dma, dma, dma,
            dma, dma((2,)), dma, dma((2, 8)),
            dma, dma((2, 2, 8)),
            dma, dma,
        ],
        compiler_params=pltpu.CompilerParams(
            collective_id=0, has_side_effects=True, vmem_limit_bytes=56 * 1024 * 1024
        ),
        name="layer",
    )(
        lengths, hidden_in, query_nope, query_rope, new_latent, key_absorb, value_absorb, output_proj,
        norm_gain.reshape(1, -1), router_proj, expert_ids, block_table, subtree_moves,
        latent_cache, expert_gate, expert_up, expert_down,
    )


def solution(mesh):
    in_specs = (
        P("ep", None), P("ep", "grp"), P("ep", "grp"), P("ep", None), P("ep", None),
        P("grp", None, None), P("grp", None, None), P("grp", None), P(), P(), P("ep", None),
        P("ep", None, "grp"), P("ep", None, "grp"), P("ep", "grp", None), P("ep", None), P("ep"),
        P("ep", None, None),
    )
    return jax.shard_map(local, mesh=mesh, in_specs=in_specs, out_specs=P("ep", "grp"), check_vma=False)
```

```python
import jax
import jax.numpy as jnp
from jax import lax
from jax.experimental import pallas as pl
from jax.experimental.pallas import tpu as pltpu
from jax.sharding import PartitionSpec as P

BF = jnp.bfloat16
F32 = jnp.float32
MESH = pl.DeviceIdType.MESH
NG = 8
NE = 64
NEG = -1e30


def iota(shape, dim):
    return lax.broadcasted_iota(jnp.int32, shape, dim)


def hot(condition):
    return jnp.where(condition, 1.0, 0.0).astype(BF)


def dot(a, b):
    return jnp.dot(a, b, preferred_element_type=F32)


def dot_nt(a, b):
    return lax.dot_general(a, b, (((1,), (1,)), ((), ())), preferred_element_type=F32)


def dot_tn(a, b):
    return lax.dot_general(a, b, (((0,), (0,)), ((), ())), preferred_element_type=F32)


def await_bytes(ref, sem):
    pltpu.make_async_copy(ref, ref, sem).wait()


def kernel(
    len_ref, hid, qn, qr, nl, ka, va, op, gain, router, ids, bt, mv, cache_hbm, wg_hbm, wu_hbm, wd_hbm,
    out,
    wg, wu, wd, msg, far, pool, qe, qo, use, m_ref, l_ref, acc_e, acc_o, p3s, p3r, p4s, p4r, lgs, lgr, st, xs, gath,
    acc_g, acc_u, act, part, rsr, ys, ret,
    cache_sem, w_sem, e1s, e1r, n1s, n1r, a1s, a1r, p3ss, p3rs, p4ss, p4rs, lgss, lgrs, e2s, e2r, a2s, a2r, rss, rsrs, e3s, e3r,
):
    g = lax.axis_index("grp")
    me = lax.axis_index("ep")
    scale = (128 + 64) ** (-0.5)
    sent = []

    def peer(k):
        return lax.rem(g + (k + NG), NG)

    def loop(lo, hi, body):
        def step(i, carry):
            body(i)
            return carry

        lax.fori_loop(lo, hi, step, 0)

    barrier = pltpu.get_barrier_semaphore()
    loop(1, NE, lambda k: pl.semaphore_signal(
        barrier, inc=1, device_id={"ep": lax.rem(me + k, NE)}, device_id_type=MESH))
    loop(1, NG, lambda k: pl.semaphore_signal(barrier, inc=1, device_id={"grp": peer(k)}, device_id_type=MESH))

    cache = pool.at[pl.ds(3, 4)]
    for p in range(8):
        pltpu.make_async_copy(
            cache_hbm.at[:, pl.ds(1152 * p, 1152)], pool.at[3 + p // 2, pl.ds(64 * (p % 2), 64)], cache_sem
        ).start()
    w_copies = [
        pltpu.make_async_copy(wg_hbm, wg, w_sem.at[0]),
        pltpu.make_async_copy(wu_hbm, wu, w_sem.at[1]),
        pltpu.make_async_copy(wd_hbm.at[0], wd, w_sem.at[2]),
    ]
    for copy in w_copies:
        copy.start()

    z = (me // 2) % 8
    xc = (me // 16) * 2 + me % 2

    def rank(xc_, z_):
        return (xc_ // 2) * 16 + z_ * 2 + xc_ % 2

    await_bytes(cache, cache_sem)

    def build(k):
        row = iota((128, 64), 0)
        slot_ = row // 16
        to_far = jnp.where(slot_ < 5, rank(lax.rem(g - xc + 8, 8), lax.rem(z + 2 + slot_, 8)), -1)
        to_near = rank(slot_, lax.rem(z + k + 7, 8))
        sel = hot(iota((128, 64), 1) == jnp.where(k == 3, to_far, to_near))
        picked = dot_nt(sel, mv[...].astype(F32).astype(BF))
        rk = iota((128, 1), 0)
        blk = jnp.where((rk // 8) % 2 == 0, picked[:, 0:1], picked[:, 1:2])
        code = jnp.where(blk < -0.5, -1.0, blk + (64 * (rk % 8)).astype(F32)).astype(jnp.int32)
        big = hot(iota((128, 512), 1) == code)
        msg[k] = dot(big, cache[...].reshape(512, 1152)).astype(BF).reshape(8, 16, 1152)

    build(3)
    pl.semaphore_wait(barrier, NE - 1 + NG - 1)

    loop(0, 5, lambda j: pltpu.make_async_remote_copy(
        msg.at[3, j], far.at[g, pl.ds(pl.multiple_of(16 * j, 16), 16)], e1s, e1r.at[j // 3],
        device_id={"ep": rank(lax.rem(g - xc + 8, 8), lax.rem(z + 2 + j, 8))}, device_id_type=MESH,
    ).start())
    sent.append(lambda: await_bytes(msg.at[3, pl.ds(0, 5)], e1s))
    loop(0, 3, build)

    def move_near(k):
        def one(j):
            to = rank(j, lax.rem(z + k + 7, 8))
            there = pool.at[k, pl.ds(pl.multiple_of(16 * xc, 16), 16)]

            @pl.when(to == me)
            def _():
                pltpu.make_async_copy(msg.at[k, j], there, n1r.at[k]).start()

            @pl.when(to != me)
            def _():
                pltpu.make_async_remote_copy(
                    msg.at[k, j], there, n1s.at[k], n1r.at[k], device_id={"ep": to}, device_id_type=MESH
                ).start()

        loop(0, 8, one)

    for h in range(2):
        rows = pl.ds(64 * h, 64)
        q_lat = dot(qn[:, 128 * h : 128 * h + 128], ka[h]).astype(BF)
        a, b = iota((128, 128), 0), iota((128, 128), 1)
        rope = dot(qr[...], hot((b < 64) & (a == b + 64 * h))).astype(BF)
        qe[rows, 0:512] = q_lat
        qe[rows, 512:640] = rope
    qo[...] = dot(qe[...], hot(iota((640, 640), 1) == iota((640, 640), 0) + 64)).astype(BF)

    req = iota((16, 64), 0)
    lens = jnp.zeros((16, 64), jnp.int32)
    for i in range(16):
        lens = jnp.where(req == i, len_ref[i], lens)
    count = jnp.clip(lens - 16 * iota((16, 64), 1), 0, 16)
    table = bt[...]
    addr = iota((16, 192), 1)
    usable = jnp.zeros((16, 192), jnp.int32)
    for p in range(64):
        usable = usable + jnp.where(table[:, p : p + 1] == addr, count[:, p : p + 1], 0)
    lam = iota((128, 16), 0)
    spread = hot((lam % 64) // 4 == iota((128, 16), 1))
    use[...] = dot(spread, usable.astype(F32).astype(BF)).astype(BF)

    pool[7, 0:16] = nl[:, 0:1152]
    pool[7, 16:32] = nl[:, 1152:2304]
    pool[7, 32:128] = jnp.zeros((96, 1152), BF)

    acc_e[...] = jnp.zeros_like(acc_e)
    acc_o[...] = jnp.zeros_like(acc_o)
    m_ref[...] = jnp.full_like(m_ref, NEG)
    l_ref[...] = jnp.zeros_like(l_ref)

    def attend(parts):
        scores = []
        m = m_ref[...]
        m_new = m
        for x, c in parts:
            s_e = jnp.where(c > 0.5, dot_nt(qe[...], x[:, 0:640]) * scale, NEG)
            s_o = jnp.where(c > 1.5, dot_nt(qo[...], x[:, 512:1152]) * scale, NEG)
            m_new = jnp.maximum(m_new, jnp.max(jnp.maximum(s_e, s_o), axis=1, keepdims=True))
            scores.append((s_e, s_o))
        f = jnp.exp(m - m_new)
        l = l_ref[...] * f
        out_e = acc_e[...] * f
        out_o = acc_o[...] * f
        for (x, c), (s_e, s_o) in zip(parts, scores):
            p_e = jnp.where(c > 0.5, jnp.exp(s_e - m_new), 0.0)
            p_o = jnp.where(c > 1.5, jnp.exp(s_o - m_new), 0.0)
            l = l + jnp.sum(p_e + p_o, axis=1, keepdims=True)
            out_e = out_e + dot(p_e.astype(BF), x[:, 0:512])
            out_o = out_o + dot(p_o.astype(BF), x[:, 512:1152])
        m_ref[...] = m_new
        l_ref[...] = l
        acc_e[...] = out_e
        acc_o[...] = out_o

    def far_part(o):
        col = iota((192, 80), 1)
        source = rank(lax.rem(o - xc + 8, 8), lax.rem(z + 14 - col // 16, 8))
        place = hot(iota((192, 80), 0) == 64 + 2 * source + (col // 8) % 2)
        return far[o], dot(use[...], place) - (2 * (iota((128, 80), 1) % 8)).astype(F32)

    def attend_pool(i):
        col = iota((192, 128), 1)
        moved = 64 + 2 * rank(col // 16, lax.rem(z + 9 - i, 8)) + (col // 8) % 2
        place = jnp.where(i < 3, moved, col % 64)
        lam, key = iota((128, 128), 0), iota((128, 128), 1)
        pair = jnp.where(i < 3, key % 8, 2 * (i - 3) + key // 64)
        c = dot(use[...], hot(iota((192, 128), 0) == place)) - (2 * pair).astype(F32)
        fresh = jnp.where(((lam % 64) // 4 == key % 16) & (key < 32), lam % 4 + 1 - 2 * (key // 16), 0)
        attend([(pool[i], jnp.where(i == 7, fresh.astype(F32), c))])

    loop(0, 5, lambda q: attend_pool(7 - q))

    def ring_part(at, ssem, rsem, h):
        up = 1 - 2 * h

        def send(o, way):
            pltpu.make_async_remote_copy(
                at(o, h), at(o, h), ssem, rsem.at[h, o], device_id={"grp": peer(way)}, device_id_type=MESH
            ).start()

        def own():
            send(g, up)
            send(g, -up)

        def forward(t):
            a, b = peer(-up * t), peer(up * t)
            await_bytes(at(a, h), rsem.at[h, a])

            @pl.when(t < 4)
            def _():
                send(a, up)
                await_bytes(at(b, h), rsem.at[h, b])

                @pl.when(t < 3)
                def _():
                    send(b, -up)

        return own, forward

    def far_half(o, h):
        return far.at[o, pl.ds(48 * h, 48 - 16 * h)]

    own_0, forward_0 = ring_part(far_half, a1s, a1r, 0)
    own_1, forward_1 = ring_part(far_half, a1s, a1r, 1)
    await_bytes(far_half(g, 0), e1r.at[0])
    own_0()
    await_bytes(far_half(g, 1), e1r.at[1])
    own_1()
    loop(0, 3, move_near)
    sent.append(lambda: await_bytes(msg.at[0], n1s.at[0]))
    sent.append(lambda: await_bytes(msg.at[1, pl.ds(0, 7)], n1s.at[1]))
    sent.append(lambda: await_bytes(msg.at[2], n1s.at[2]))
    attend([far_part(g)])

    def step_far(t):
        forward_0(t)
        forward_1(t)

        @pl.when(t < 4)
        def _():
            attend([far_part(peer(-t)), far_part(peer(t))])

        @pl.when(t > 1)
        def _():
            k = lax.rem(t + 2, 3)
            await_bytes(pool.at[k], n1r.at[k])
            attend_pool(k)

    loop(1, 5, step_far)
    attend([far_part(peer(4))])
    sent.append(lambda: await_bytes(far.at[pl.ds(0, 7)], a1s))
    total = acc_e[...] + acc_o[...][:, 64:576]
    latent = (total / l_ref[...]).astype(BF)
    heads = [dot(latent[64 * h : 64 * h + 64], va[h]).astype(BF) for h in range(2)]
    term = dot(heads[0], op[0:128]) + dot(heads[1], op[128:256])
    for c in range(8):
        p3s[c] = term[:, 256 * c : 256 * c + 256].astype(BF)

    def exchange(src, dst, ssem, rsem):
        loop(1, NG, lambda k: pltpu.make_async_remote_copy(
            src(peer(k)), dst.at[k - 1], ssem, rsem, device_id={"grp": peer(k)}, device_id_type=MESH
        ).start())

    exchange(lambda c: p3s.at[c], p3r, p3ss, p3rs)
    sent.append(lambda: await_bytes(p3s.at[pl.ds(0, 7)], p3ss))
    ids_v = ids[...]
    expert = iota((64, 64), 0)
    named_t = jnp.zeros((64, 64), F32)
    for k in range(6):
        named_t = named_t + jnp.where(ids_v[k : k + 1, :] == expert, 1.0, 0.0)
    identity = hot(iota((64, 64), 0) == iota((64, 64), 1))
    named_b = dot_nt(identity, named_t.astype(BF)).astype(BF)
    before = dot(hot(iota((64, 64), 1) < iota((64, 64), 0)), named_b).astype(BF)
    widen = hot(iota((64, 512), 1) // 8 == iota((64, 512), 0))
    slot = (iota((64, 512), 1) % 8).astype(F32)
    chosen = (dot(named_b, widen) > 0.5) & (jnp.abs(dot(before, widen) - slot) < 0.5)
    chosen_b = hot(chosen)

    await_bytes(p3r, p3rs)
    cols = pl.ds(pl.multiple_of(g * 256, 256), 256)
    attn = p3s[g].astype(F32)
    for k in range(NG - 1):
        attn = attn + p3r[k].astype(F32)
    state = hid[:, cols].astype(F32) + attn
    st[...] = state
    square = jnp.sum(state * state, axis=1, keepdims=True)
    diagonal = iota((64, 128), 0) == iota((64, 128), 1)
    p4s[...] = jnp.broadcast_to(jnp.sum(jnp.where(diagonal, square, 0.0), axis=0, keepdims=True), (8, 128))
    exchange(lambda c: p4s, p4r, p4ss, p4rs)
    sent.append(lambda: await_bytes(p4r, p4ss))
    await_bytes(p4r, p4rs)
    squares = p4s[...]
    for k in range(NG - 1):
        squares = squares + p4r[k]
    square = jnp.sum(jnp.where(diagonal, squares[0:1], 0.0), axis=1, keepdims=True)
    inverse = lax.rsqrt(square / 2048.0 + 1e-06)
    normed = (state * inverse * gain[:, cols].astype(F32)).astype(BF)

    xs[...] = dot_tn(chosen_b, normed).reshape(64, 8, 256).astype(BF)

    def dispatch(n):
        to = rank(lax.rem(n + xc, 8), lax.rem(z + 2 + n // 8, 8))
        there = gath.at[g, 8 * (n // 8) + xc]
        sem = e2r.at[n // 40]

        @pl.when(to == me)
        def _():
            pltpu.make_async_copy(xs.at[me], there, sem).start()

        @pl.when(to != me)
        def _():
            pltpu.make_async_remote_copy(
                xs.at[to], there, e2s, sem, device_id={"ep": to}, device_id_type=MESH
            ).start()

    loop(0, NE, dispatch)
    lgs[...] = dot_nt(normed, router[:, cols])
    exchange(lambda c: lgs, lgr, lgss, lgrs)
    sent.append(lambda: await_bytes(lgr, lgss))
    sent.append(lambda: await_bytes(xs.at[pl.ds(0, 63)], e2s))
    for copy in w_copies:
        copy.wait()
    acc_g[...] = jnp.zeros_like(acc_g)
    acc_u[...] = jnp.zeros_like(acc_u)

    def half(h):
        return pl.ds(40 * h, 40 - 16 * h)

    def rows_of(h):
        return pl.ds(320 * h, 320 - 128 * h)

    def gath_half(o, h):
        return gath.at[o, half(h)]

    def expert_columns(o, h):
        x = gath[o, half(h)].reshape(320 - 128 * h, 256)
        lanes = pl.ds(pl.multiple_of(o * 256, 256), 256)
        acc_g[rows_of(h), :] += dot_nt(x, wg[:, lanes])
        acc_u[rows_of(h), :] += dot_nt(x, wu[:, lanes])

    def both_sides(t, h):
        loop(0, jnp.where(t < 4, 2, 1), lambda i: expert_columns(peer(t * (2 * i - 1)), h))

    def activate(h):
        gate = acc_g[rows_of(h), :]
        act[rows_of(h), :] = (gate / (1.0 + jnp.exp(-gate)) * acc_u[rows_of(h), :]).astype(BF)

    def pass_on(c, h, way):
        d = (1 - way) // 2
        pltpu.make_async_remote_copy(
            part.at[c, half(h)], rsr.at[d, c, half(h)], rss, rsrs.at[d, h, c],
            device_id={"grp": peer(way)}, device_id_type=MESH,
        ).start()

    def make(h):
        up = 1 - 2 * h

        def one(i):
            near = 4 - (i + 1) // 2
            c = peer(jnp.where(i % 2 == 1, -up * near, up * near))
            lanes = pl.ds(pl.multiple_of(c * 256, 256), 256)
            part[c, half(h)] = dot(act[rows_of(h), :], wd[:, lanes]).reshape(40 - 16 * h, 8, 256).astype(BF)

            @pl.when(i == 0)
            def _():
                pass_on(c, h, up)

            @pl.when(i == 1)
            def _():
                pass_on(c, h, -up)

        loop(0, 8, one)

    def add_on(t, h):
        up = 1 - 2 * h

        def stream(i):
            way = up * (1 - 2 * i)
            c = peer(way * (4 - i - t))
            d = (1 - way) // 2
            await_bytes(rsr.at[d, c, half(h)], rsrs.at[d, h, c])
            part[c, half(h)] = (part[c, half(h)].astype(F32) + rsr[d, c, half(h)].astype(F32)).astype(BF)
            pass_on(c, h, way)

        loop(0, jnp.where(t < 3, 2, 1), stream)

    def own_half(h):
        total_h = part[g, half(h)].astype(F32)
        for d in range(2):
            await_bytes(rsr.at[d, g, half(h)], rsrs.at[d, h, g])
            total_h = total_h + rsr[d, g, half(h)].astype(F32)
        ys[half(h)] = total_h.astype(BF)

    def give_back(n):
        to = rank(lax.rem(n + xc, 8), lax.rem(z + 14 - n // 8, 8))
        here = ys.at[8 * (n // 8) + lax.rem(n + xc, 8)]

        @pl.when(to == me)
        def _():
            pltpu.make_async_copy(here, ret.at[me], e3r).start()

        @pl.when(to != me)
        def _():
            pltpu.make_async_remote_copy(
                here, ret.at[me], e3s, e3r, device_id={"ep": to}, device_id_type=MESH
            ).start()

    own_0, forward_0 = ring_part(gath_half, a2s, a2r, 0)
    own_1, forward_1 = ring_part(gath_half, a2s, a2r, 1)
    await_bytes(gath_half(g, 0), e2r.at[0])
    own_0()
    expert_columns(g, 0)

    await_bytes(gath_half(g, 1), e2r.at[1])
    own_1()
    expert_columns(g, 1)

    def step_expert(t):
        forward_0(t)
        forward_1(t)
        for h in range(2):
            both_sides(t, h)

    loop(1, 4, step_expert)
    forward_0(4)
    expert_columns(peer(4), 0)
    activate(0)
    make(0)
    forward_1(4)
    expert_columns(peer(4), 1)
    sent.append(lambda: await_bytes(gath.at[pl.ds(0, 7)], a2s))
    activate(1)
    make(1)

    def step_sum(t):
        add_on(t, 0)
        add_on(t, 1)

    loop(1, 4, step_sum)
    own_half(0)
    loop(0, 40, give_back)
    own_half(1)
    sent.append(lambda: await_bytes(part.at[pl.ds(0, 7)], rss))
    loop(40, NE, give_back)
    sent.append(lambda: await_bytes(ys.at[pl.ds(0, 63)], e3s))

    await_bytes(lgr, lgrs)
    logits = lgs[...]
    for k in range(NG - 1):
        logits = logits + lgr[k]
    weight = jnp.where(named_b.astype(F32) > 0.5, jax.nn.sigmoid(logits), 0.0)
    weight = weight / jnp.sum(weight, axis=1, keepdims=True)
    w_hi = weight.astype(BF)
    w_lo = (weight - w_hi.astype(F32)).astype(BF)
    mask = chosen_b.astype(F32)
    mix_hi = (dot(w_hi, widen) * mask).astype(BF)
    mix_lo = (dot(w_lo, widen) * mask).astype(BF)
    await_bytes(ret, e3r)
    results = ret[...].reshape(512, 256)
    out[...] = (st[...] + dot(mix_hi, results) + dot(mix_lo, results)).astype(BF)

    for wait in sent:
        wait()


def local(
    hidden_in, query_nope, query_rope, new_latent, latent_cache, key_absorb, value_absorb, output_proj, norm_gain,
    router_proj, expert_ids, expert_gate, expert_up, expert_down, block_table, lengths, subtree_moves,
):
    vmem = pl.BlockSpec(memory_space=pltpu.VMEM)
    anywhere = pl.BlockSpec(memory_space=pl.ANY)
    dma = pltpu.SemaphoreType.DMA
    v = pltpu.VMEM
    return pl.pallas_call(
        kernel,
        out_shape=jax.ShapeDtypeStruct((64, 256), BF),
        in_specs=[pl.BlockSpec(memory_space=pltpu.SMEM)] + [vmem] * 12 + [anywhere] * 4,
        out_specs=vmem,
        scratch_shapes=[
            v((176, 2048), BF),
            v((176, 2048), BF),
            v((176, 2048), BF),
            v((4, 8, 16, 1152), BF),
            v((8, 80, 1152), BF),
            v((8, 128, 1152), BF),
            v((128, 640), BF),
            v((128, 640), BF),
            v((128, 192), BF),
            v((128, 1), F32),
            v((128, 1), F32),
            v((128, 512), F32),
            v((128, 640), F32),
            v((8, 64, 256), BF),
            v((7, 64, 256), BF),
            v((8, 128), F32),
            v((7, 8, 128), F32),
            v((64, 64), F32),
            v((7, 64, 64), F32),
            v((64, 256), F32),
            v((64, 8, 256), BF),
            v((8, 64, 8, 256), BF),
            v((512, 176), F32),
            v((512, 176), F32),
            v((512, 176), BF),
            v((8, 64, 8, 256), BF),
            v((2, 8, 64, 8, 256), BF),
            v((64, 8, 256), BF),
            v((64, 8, 256), BF),
            dma, dma((3,)),
            dma, dma((2,)), dma((3,)), dma((3,)), dma, dma((2, 8)),
            dma, dma, dma, dma, dma, dma,
            dma, dma((2,)), dma, dma((2, 8)),
            dma, dma((2, 2, 8)),
            dma, dma,
        ],
        compiler_params=pltpu.CompilerParams(
            collective_id=0, has_side_effects=True, vmem_limit_bytes=56 * 1024 * 1024
        ),
        name="layer",
    )(
        lengths, hidden_in, query_nope, query_rope, new_latent, key_absorb, value_absorb, output_proj,
        norm_gain.reshape(1, -1), router_proj.T, expert_ids.T, block_table, subtree_moves[0].T,
        latent_cache, expert_gate[0].T, expert_up[0].T, expert_down,
    )


def solution(mesh):
    in_specs = (
        P("ep", None), P("ep", "grp"), P("ep", "grp"), P("ep", None), P("ep", None),
        P("grp", None, None), P("grp", None, None), P("grp", None), P(), P(), P("ep", None),
        P("ep", None, "grp"), P("ep", None, "grp"), P("ep", "grp", None), P("ep", None), P("ep"),
        P("ep", None, None),
    )
    return jax.shard_map(local, mesh=mesh, in_specs=in_specs, out_specs=P("ep", "grp"), check_vma=False)
```

```python
import jax
import jax.numpy as jnp
from jax import lax
from jax.experimental import pallas as pl
from jax.experimental.pallas import tpu as pltpu
from jax.sharding import PartitionSpec as P

BF = jnp.bfloat16
F32 = jnp.float32
MESH = pl.DeviceIdType.MESH
NG = 8
NE = 64
NEG = -1e30


def iota(shape, dim):
    return lax.broadcasted_iota(jnp.int32, shape, dim)


def hot(condition):
    return jnp.where(condition, 1.0, 0.0).astype(BF)


def dot(a, b):
    return jnp.dot(a, b, preferred_element_type=F32)


def dot_nt(a, b):
    return lax.dot_general(a, b, (((1,), (1,)), ((), ())), preferred_element_type=F32)


def dot_tn(a, b):
    return lax.dot_general(a, b, (((0,), (0,)), ((), ())), preferred_element_type=F32)


def await_bytes(ref, sem):
    pltpu.make_async_copy(ref, ref, sem).wait()


def kernel(
    len_ref, qn, qr, ka, gain, ids, bt, mv, hid_hbm, nl_hbm, va_hbm, op_hbm, router_hbm, cache_hbm, wg_hbm, wu_hbm, wd_hbm,
    out,
    hid, nl, va, op, router, wg, wu, wd, msg, far, pool, qe, qo, use, m_ref, l_ref, acc_e, acc_o, p3s, p3r, p4s, p4r, nrm, st, xs, gath, xn, gn,
    acc_g, acc_u, act, part, rsr, ys, ret, yn, rn, mns, mnr,
    cache_sem, w_sem, e1s, e1r, n1s, n1r, a1s, a1r, p3ss, p3rs, p4ss, p4rs, nxs, nxr, e2s, e2r, n2s, n2r, a2s, a2r, rss, rsrs, e3s, e3r, n3s, n3r, mxs, mxr,
):
    g = lax.axis_index("grp")
    me = lax.axis_index("ep")
    scale = (128 + 64) ** (-0.5)
    sent = []

    def peer(k):
        return lax.rem(g + (k + NG), NG)

    def loop(lo, hi, body):
        def step(i, carry):
            body(i)
            return carry

        lax.fori_loop(lo, hi, step, 0)

    barrier = pltpu.get_barrier_semaphore()
    loop(1, NE, lambda k: pl.semaphore_signal(
        barrier, inc=1, device_id={"ep": lax.rem(me + k, NE)}, device_id_type=MESH))
    loop(1, NG, lambda k: pl.semaphore_signal(barrier, inc=1, device_id={"grp": peer(k)}, device_id_type=MESH))

    cache = pool.at[pl.ds(3, 4)]
    for p in range(8):
        pltpu.make_async_copy(
            cache_hbm.at[:, pl.ds(1152 * p, 1152)], pool.at[3 + p // 2, pl.ds(64 * (p % 2), 64)], cache_sem
        ).start()
    w_copies = [
        pltpu.make_async_copy(wg_hbm, wg, w_sem.at[0]),
        pltpu.make_async_copy(wu_hbm, wu, w_sem.at[1]),
        pltpu.make_async_copy(wd_hbm.at[0], wd, w_sem.at[2]),
    ]
    o_copies = [
        pltpu.make_async_copy(nl_hbm, nl, w_sem.at[3]),
        pltpu.make_async_copy(va_hbm, va, w_sem.at[4]),
        pltpu.make_async_copy(op_hbm, op, w_sem.at[5]),
        pltpu.make_async_copy(hid_hbm, hid, w_sem.at[6]),
        pltpu.make_async_copy(router_hbm, router, w_sem.at[7]),
    ]
    for copy in o_copies:
        copy.start()
    for copy in w_copies:
        copy.start()

    z = (me // 2) % 8
    xc = (me // 16) * 2 + me % 2

    def rank(xc_, z_):
        return (xc_ // 2) * 16 + z_ * 2 + xc_ % 2

    def away(j):
        return jnp.where(j > 4, 2 + j, jnp.where(j % 2 == 0, 2 + j // 2, 6 - j // 2))

    def ahead(j):
        return lax.rem(z + away(j), 8)

    def behind(j):
        return lax.rem(z + 16 - away(j), 8)

    await_bytes(cache, cache_sem)

    def build(k):
        row = iota((128, 64), 0)
        slot_ = row // 16
        to_far = jnp.where(slot_ < 5, rank(lax.rem(g - xc + 8, 8), ahead(slot_)), -1)
        to_near = rank(slot_, lax.rem(z + k + 7, 8))
        sel = hot(iota((128, 64), 1) == jnp.where(k == 3, to_far, to_near))
        picked = dot_nt(sel, mv[...].astype(F32).astype(BF))
        rk = iota((128, 1), 0)
        blk = jnp.where((rk // 8) % 2 == 0, picked[:, 0:1], picked[:, 1:2])
        code = jnp.where(blk < -0.5, -1.0, blk + (64 * (rk % 8)).astype(F32)).astype(jnp.int32)
        big = hot(iota((128, 512), 1) == code)
        msg[k] = dot(big, cache[...].reshape(512, 1152)).astype(BF).reshape(8, 16, 1152)

    build(3)
    pl.semaphore_wait(barrier, NE - 1 + NG - 1)

    loop(0, 5, lambda j: pltpu.make_async_remote_copy(
        msg.at[3, j], far.at[g, pl.ds(pl.multiple_of(16 * j, 16), 16)], e1s, e1r.at[j // 3],
        device_id={"ep": rank(lax.rem(g - xc + 8, 8), ahead(j))}, device_id_type=MESH,
    ).start())
    sent.append(lambda: await_bytes(msg.at[3, pl.ds(0, 5)], e1s))
    loop(0, 3, build)

    def move_near(k):
        def one(j):
            to = rank(j, lax.rem(z + k + 7, 8))
            there = pool.at[k, pl.ds(pl.multiple_of(16 * xc, 16), 16)]

            @pl.when(to == me)
            def _():
                pltpu.make_async_copy(msg.at[k, j], there, n1r.at[k]).start()

            @pl.when(to != me)
            def _():
                pltpu.make_async_remote_copy(
                    msg.at[k, j], there, n1s.at[k], n1r.at[k], device_id={"ep": to}, device_id_type=MESH
                ).start()

        loop(0, 8, one)

    for h in range(2):
        rows = pl.ds(64 * h, 64)
        q_lat = dot(qn[:, 128 * h : 128 * h + 128], ka[h]).astype(BF)
        a, b = iota((128, 128), 0), iota((128, 128), 1)
        rope = dot(qr[...], hot((b < 64) & (a == b + 64 * h))).astype(BF)
        qe[rows, 0:512] = q_lat
        qe[rows, 512:640] = rope
    qo[...] = dot(qe[...], hot(iota((640, 640), 1) == iota((640, 640), 0) + 64)).astype(BF)

    req = iota((16, 64), 0)
    lens = jnp.zeros((16, 64), jnp.int32)
    for i in range(16):
        lens = jnp.where(req == i, len_ref[i], lens)
    count = jnp.clip(lens - 16 * iota((16, 64), 1), 0, 16)
    table = bt[...]
    addr = iota((16, 192), 1)
    usable = jnp.zeros((16, 192), jnp.int32)
    for p in range(64):
        usable = usable + jnp.where(table[:, p : p + 1] == addr, count[:, p : p + 1], 0)
    lam = iota((128, 16), 0)
    spread = hot((lam % 64) // 4 == iota((128, 16), 1))
    use[...] = dot(spread, usable.astype(F32).astype(BF)).astype(BF)

    for copy in o_copies:
        copy.wait()
    pool[7, 0:16] = nl[:, 0:1152]
    pool[7, 16:32] = nl[:, 1152:2304]
    pool[7, 32:128] = jnp.zeros((96, 1152), BF)

    acc_e[...] = jnp.zeros_like(acc_e)
    acc_o[...] = jnp.zeros_like(acc_o)
    m_ref[...] = jnp.full_like(m_ref, NEG)
    l_ref[...] = jnp.zeros_like(l_ref)

    def attend(parts):
        scores = []
        m = m_ref[...]
        m_new = m
        for x, c in parts:
            s_e = jnp.where(c > 0.5, dot_nt(qe[...], x[:, 0:640]) * scale, NEG)
            s_o = jnp.where(c > 1.5, dot_nt(qo[...], x[:, 512:1152]) * scale, NEG)
            m_new = jnp.maximum(m_new, jnp.max(jnp.maximum(s_e, s_o), axis=1, keepdims=True))
            scores.append((s_e, s_o))
        f = jnp.exp(m - m_new)
        l = l_ref[...] * f
        out_e = acc_e[...] * f
        out_o = acc_o[...] * f
        for (x, c), (s_e, s_o) in zip(parts, scores):
            p_e = jnp.where(c > 0.5, jnp.exp(s_e - m_new), 0.0)
            p_o = jnp.where(c > 1.5, jnp.exp(s_o - m_new), 0.0)
            l = l + jnp.sum(p_e + p_o, axis=1, keepdims=True)
            out_e = out_e + dot(p_e.astype(BF), x[:, 0:512])
            out_o = out_o + dot(p_o.astype(BF), x[:, 512:1152])
        m_ref[...] = m_new
        l_ref[...] = l
        acc_e[...] = out_e
        acc_o[...] = out_o

    def far_part(o):
        col = iota((192, 80), 1)
        source = rank(lax.rem(o - xc + 8, 8), behind(col // 16))
        place = hot(iota((192, 80), 0) == 64 + 2 * source + (col // 8) % 2)
        return far[o], dot(use[...], place) - (2 * (iota((128, 80), 1) % 8)).astype(F32)

    def attend_pool(i):
        col = iota((192, 128), 1)
        moved = 64 + 2 * rank(col // 16, lax.rem(z + 9 - i, 8)) + (col // 8) % 2
        place = jnp.where(i < 3, moved, col % 64)
        lam, key = iota((128, 128), 0), iota((128, 128), 1)
        pair = jnp.where(i < 3, key % 8, 2 * (i - 3) + key // 64)
        c = dot(use[...], hot(iota((192, 128), 0) == place)) - (2 * pair).astype(F32)
        fresh = jnp.where(((lam % 64) // 4 == key % 16) & (key < 32), lam % 4 + 1 - 2 * (key // 16), 0)
        attend([(pool[i], jnp.where(i == 7, fresh.astype(F32), c))])

    loop(0, 5, lambda q: attend_pool(7 - q))

    def ring_part(at, ssem, rsem, h):
        up = 1 - 2 * h

        def send(o, way):
            pltpu.make_async_remote_copy(
                at(o, h), at(o, h), ssem, rsem.at[h, o], device_id={"grp": peer(way)}, device_id_type=MESH
            ).start()

        def own():
            send(g, up)
            send(g, -up)

        def forward(t):
            a, b = peer(-up * t), peer(up * t)
            await_bytes(at(a, h), rsem.at[h, a])

            @pl.when(t < 4)
            def _():
                send(a, up)
                await_bytes(at(b, h), rsem.at[h, b])

                @pl.when(t < 3)
                def _():
                    send(b, -up)

        return own, forward

    def far_half(o, h):
        return far.at[o, pl.ds(48 * h, 48 - 16 * h)]

    own_0, forward_0 = ring_part(far_half, a1s, a1r, 0)
    own_1, forward_1 = ring_part(far_half, a1s, a1r, 1)
    await_bytes(far_half(g, 0), e1r.at[0])
    own_0()
    await_bytes(far_half(g, 1), e1r.at[1])
    own_1()
    loop(0, 3, move_near)
    sent.append(lambda: await_bytes(msg.at[0], n1s.at[0]))
    sent.append(lambda: await_bytes(msg.at[1, pl.ds(0, 7)], n1s.at[1]))
    sent.append(lambda: await_bytes(msg.at[2], n1s.at[2]))
    attend([far_part(g)])

    def step_far(t):
        forward_0(t)
        forward_1(t)

        @pl.when(t < 4)
        def _():
            attend([far_part(peer(-t)), far_part(peer(t))])

        @pl.when(t > 1)
        def _():
            k = lax.rem(t + 2, 3)
            await_bytes(pool.at[k], n1r.at[k])
            attend_pool(k)

    loop(1, 5, step_far)
    attend([far_part(peer(4))])
    sent.append(lambda: await_bytes(far.at[pl.ds(0, 7)], a1s))
    total = acc_e[...] + acc_o[...][:, 64:576]
    latent = (total / l_ref[...]).astype(BF)
    heads = [dot(latent[64 * h : 64 * h + 64], va[h]).astype(BF) for h in range(2)]
    head_out = jnp.concatenate(heads, axis=1)

    def attn_block(k):
        c = peer(k)
        p3s[c] = dot(head_out, op[:, pl.ds(pl.multiple_of(c * 256, 256), 256)]).astype(BF)

        @pl.when(k > 0)
        def _():
            pltpu.make_async_remote_copy(
                p3s.at[c], p3r.at[k - 1], p3ss, p3rs, device_id={"grp": c}, device_id_type=MESH
            ).start()

    loop(0, NG, lambda k: attn_block(NG - 1 - k))
    sent.append(lambda: await_bytes(p3s.at[pl.ds(0, 7)], p3ss))

    def exchange(src, dst, ssem, rsem):
        loop(1, NG, lambda k: pltpu.make_async_remote_copy(
            src(peer(k)), dst.at[k - 1], ssem, rsem, device_id={"grp": peer(k)}, device_id_type=MESH
        ).start())

    ids_v = ids[...]
    expert = iota((64, 64), 0)
    named_t = jnp.zeros((64, 64), F32)
    for k in range(6):
        named_t = named_t + jnp.where(ids_v[k : k + 1, :] == expert, 1.0, 0.0)
    identity = hot(iota((64, 64), 0) == iota((64, 64), 1))
    named_b = dot_nt(identity, named_t.astype(BF)).astype(BF)
    before = dot(hot(iota((64, 64), 1) < iota((64, 64), 0)), named_b).astype(BF)
    def choose(first, slots):
        col = iota((64, 8 * slots), 1)
        n = first + col // 8
        widen = hot(iota((64, 8 * slots), 0) == rank(n % 8, ahead(n // 8)))
        at_slot = jnp.abs(dot(before, widen) - (col % 8).astype(F32)) < 0.5
        return widen, hot((dot(named_b, widen) > 0.5) & at_slot)

    widen_far, chosen_far = choose(0, 40)
    widen_near, chosen_near = choose(40, 24)

    await_bytes(p3r, p3rs)
    cols = pl.ds(pl.multiple_of(g * 256, 256), 256)
    attn = p3s[g].astype(F32)
    for k in range(NG - 1):
        attn = attn + p3r[k].astype(F32)
    state = hid[:, cols].astype(F32) + attn
    st[...] = state
    square = jnp.sum(state * state, axis=1, keepdims=True)
    diagonal = iota((64, 128), 0) == iota((64, 128), 1)
    p4s[...] = jnp.broadcast_to(jnp.sum(jnp.where(diagonal, square, 0.0), axis=0, keepdims=True), (8, 128))
    exchange(lambda c: p4s, p4r, p4ss, p4rs)
    sent.append(lambda: await_bytes(p4r, p4ss))
    await_bytes(p4r, p4rs)
    squares = p4s[...]
    for k in range(NG - 1):
        squares = squares + p4r[k]
    square = jnp.sum(jnp.where(diagonal, squares[0:1], 0.0), axis=1, keepdims=True)
    inverse = lax.rsqrt(square / 2048.0 + 1e-06)
    gains = gain[...].astype(F32).reshape(16, 128)
    row = iota((16, 128), 0)
    gain_cols = jnp.concatenate(
        [jnp.sum(jnp.where(row == 2 * g + i, gains, 0.0), axis=0, keepdims=True) for i in range(2)], axis=1
    )
    normed = (state * inverse * gain_cols).astype(BF)

    nrm[g] = normed
    loop(1, NG, lambda k: pltpu.make_async_remote_copy(
        nrm.at[g], nrm.at[g], nxs, nxr, device_id={"grp": peer(k)}, device_id_type=MESH
    ).start())
    sent.append(lambda: await_bytes(nrm.at[pl.ds(0, 7)], nxs))

    xs[...] = dot_tn(chosen_far, normed).reshape(40, 8, 256).astype(BF)

    def dispatch(n):
        xt = lax.rem(n + xc, 8)
        pltpu.make_async_remote_copy(
            xs.at[8 * (n // 8) + xt], gath.at[g, 8 * (n // 8) + xc], e2s, e2r.at[n // 24],
            device_id={"ep": rank(xt, ahead(n // 8))}, device_id_type=MESH,
        ).start()

    loop(0, 40, dispatch)
    sent.append(lambda: await_bytes(xs, e2s))

    def dispatch_near():
        await_bytes(nrm.at[pl.ds(0, 7)], nxr)

        def block(o):
            xn[:, o] = dot_tn(chosen_near, nrm[o]).reshape(24, 8, 256).astype(BF)

        loop(0, 8, block)

        def one(n):
            xt = lax.rem(n + xc, 8)
            to = rank(xt, lax.rem(z + 7 + n // 8, 8))
            here, there = xn.at[8 * (n // 8) + xt], gn.at[8 * (n // 8) + xc]

            @pl.when(to == me)
            def _():
                pltpu.make_async_copy(here, there, n2r).start()

            @pl.when(to != me)
            def _():
                pltpu.make_async_remote_copy(
                    here, there, n2s, n2r, device_id={"ep": to}, device_id_type=MESH
                ).start()

        loop(0, 24, one)
        sent.append(lambda: await_bytes(xn.at[pl.ds(0, 23)], n2s))

    for copy in w_copies:
        copy.wait()
    acc_g[...] = jnp.zeros_like(acc_g)
    acc_u[...] = jnp.zeros_like(acc_u)

    def half(h):
        return pl.ds(24 * h, 24 - 8 * h)

    def rows_of(h):
        return pl.ds((0, 192, 320)[h], (192, 128, 192)[h])

    def gath_half(o, h):
        return gath.at[o, half(h)]

    def add_columns(x, o, h):
        lanes = pl.ds(pl.multiple_of(o * 256, 256), 256)
        acc_g[rows_of(h), :] += dot_nt(x, wg[:, lanes])
        acc_u[rows_of(h), :] += dot_nt(x, wu[:, lanes])

    def expert_columns(o, h):
        add_columns(gath[o, half(h)].reshape(192 - 64 * h, 256), o, h)

    def both_sides(t, h):
        loop(0, jnp.where(t < 4, 2, 1), lambda i: expert_columns(peer(t * (2 * i - 1)), h))

    def activate(h):
        gate = acc_g[rows_of(h), :]
        act[rows_of(h), :] = (gate / (1.0 + jnp.exp(-gate)) * acc_u[rows_of(h), :]).astype(BF)

    def pass_on(c, h, way):
        d = (1 - way) // 2
        pltpu.make_async_remote_copy(
            part.at[c, half(h)], rsr.at[d, c, half(h)], rss, rsrs.at[d, h, c],
            device_id={"grp": peer(way)}, device_id_type=MESH,
        ).start()

    def make(h):
        up = 1 - 2 * h

        def one(i):
            near = 4 - (i + 1) // 2
            c = peer(jnp.where(i % 2 == 1, -up * near, up * near))
            lanes = pl.ds(pl.multiple_of(c * 256, 256), 256)
            part[c, half(h)] = dot(act[rows_of(h), :], wd[:, lanes]).reshape(24 - 8 * h, 8, 256).astype(BF)

            @pl.when(i == 0)
            def _():
                pass_on(c, h, up)

            @pl.when(i == 1)
            def _():
                pass_on(c, h, -up)

        loop(0, 8, one)

    def add_on(t, h):
        up = 1 - 2 * h

        def stream(i):
            way = up * (1 - 2 * i)
            c = peer(way * (4 - i - t))
            d = (1 - way) // 2
            await_bytes(rsr.at[d, c, half(h)], rsrs.at[d, h, c])
            part[c, half(h)] = (part[c, half(h)].astype(F32) + rsr[d, c, half(h)].astype(F32)).astype(BF)
            pass_on(c, h, way)

        loop(0, jnp.where(t < 3, 2, 1), stream)

    def own_half(h):
        total_h = part[g, half(h)].astype(F32)
        for d in range(2):
            await_bytes(rsr.at[d, g, half(h)], rsrs.at[d, h, g])
            total_h = total_h + rsr[d, g, half(h)].astype(F32)
        ys[half(h)] = total_h.astype(BF)

    def give_back(n):
        xt = lax.rem(n + xc, 8)
        pltpu.make_async_remote_copy(
            ys.at[8 * (n // 8) + xt], ret.at[8 * (n // 8) + xc], e3s, e3r,
            device_id={"ep": rank(xt, behind(n // 8))}, device_id_type=MESH,
        ).start()

    def give_back_near(n):
        xt = lax.rem(n + xc, 8)
        to = rank(xt, lax.rem(z + 9 - n // 8, 8))
        here, there = yn.at[8 * (n // 8) + xt], rn.at[8 * (n // 8) + xc]

        @pl.when(to == me)
        def _():
            pltpu.make_async_copy(here, there, n3r).start()

        @pl.when(to != me)
        def _():
            pltpu.make_async_remote_copy(here, there, n3s, n3r, device_id={"ep": to}, device_id_type=MESH).start()

    own_0, forward_0 = ring_part(gath_half, a2s, a2r, 0)
    own_1, forward_1 = ring_part(gath_half, a2s, a2r, 1)
    await_bytes(gath_half(g, 0), e2r.at[0])
    own_0()
    await_bytes(gath_half(g, 1), e2r.at[1])
    own_1()
    dispatch_near()
    expert_columns(g, 0)
    expert_columns(g, 1)

    def step_expert(t):
        forward_0(t)
        forward_1(t)
        for h in range(2):
            both_sides(t, h)

    loop(1, 4, step_expert)
    forward_0(4)
    expert_columns(peer(4), 0)
    activate(0)
    forward_1(4)
    expert_columns(peer(4), 1)
    activate(1)
    make(1)
    make(0)
    sent.append(lambda: await_bytes(gath.at[pl.ds(0, 7)], a2s))

    def near_block(c):
        lanes = pl.ds(pl.multiple_of(c * 256, 256), 256)
        yn[:, c] = dot(act[rows_of(2), :], wd[:, lanes]).reshape(24, 8, 256).astype(BF)

    def step_sum(t):
        add_on(t, 1)
        add_on(t, 0)

        @pl.when(t == 1)
        def _():
            await_bytes(gn, n2r)
            loop(0, 8, lambda o: add_columns(gn[:, o].reshape(192, 256), o, 2))
            activate(2)
            loop(0, 8, near_block)
            loop(0, 24, give_back_near)

    loop(1, 4, step_sum)
    sent.append(lambda: await_bytes(yn.at[pl.ds(0, 23)], n3s))
    own_half(1)
    loop(24, 40, give_back)
    own_half(0)
    loop(0, 24, give_back)
    sent.append(lambda: await_bytes(part.at[pl.ds(0, 7)], rss))
    sent.append(lambda: await_bytes(ys, e3s))

    logits = jnp.zeros((64, 64), F32)
    for o in range(8):
        logits = logits + dot_nt(nrm[o], router[:, 256 * o : 256 * o + 256])
    weight = jnp.where(named_b.astype(F32) > 0.5, jax.nn.sigmoid(logits), 0.0)
    weight = weight / jnp.sum(weight, axis=1, keepdims=True)
    w_hi = weight.astype(BF)
    w_lo = (weight - w_hi.astype(F32)).astype(BF)

    def mixer(widen, chosen):
        mask = chosen.astype(F32)
        return (dot(w_hi, widen) * mask).astype(BF), (dot(w_lo, widen) * mask).astype(BF)

    near_hi, near_lo = mixer(widen_near, chosen_near)
    far_hi, far_lo = mixer(widen_far, chosen_far)
    await_bytes(rn, n3r)
    for c in range(8):
        results = rn[:, c].reshape(192, 256)
        mns[c] = (dot(near_hi, results) + dot(near_lo, results)).astype(BF)
    exchange(lambda c: mns.at[c], mnr, mxs, mxr)
    sent.append(lambda: await_bytes(mnr, mxs))
    await_bytes(ret, e3r)
    results = ret[...].reshape(320, 256)
    total = st[...] + dot(far_hi, results) + dot(far_lo, results) + mns[g].astype(F32)
    await_bytes(mnr, mxr)
    for k in range(NG - 1):
        total = total + mnr[k].astype(F32)
    out[...] = total.astype(BF)

    for wait in sent:
        wait()


def local(
    hidden_in, query_nope, query_rope, new_latent, latent_cache, key_absorb, value_absorb, output_proj, norm_gain,
    router_proj, expert_ids, expert_gate, expert_up, expert_down, block_table, lengths, subtree_moves,
):
    vmem = pl.BlockSpec(memory_space=pltpu.VMEM)
    anywhere = pl.BlockSpec(memory_space=pl.ANY)
    dma = pltpu.SemaphoreType.DMA
    v = pltpu.VMEM
    return pl.pallas_call(
        kernel,
        out_shape=jax.ShapeDtypeStruct((64, 256), BF),
        in_specs=[pl.BlockSpec(memory_space=pltpu.SMEM)] + [vmem] * 7 + [anywhere] * 9,
        out_specs=vmem,
        scratch_shapes=[
            v((64, 2048), BF),
            v((16, 2304), BF),
            v((2, 512, 128), BF),
            v((256, 2048), BF),
            v((64, 2048), BF),
            v((176, 2048), BF),
            v((176, 2048), BF),
            v((176, 2048), BF),
            v((4, 8, 16, 1152), BF),
            v((8, 80, 1152), BF),
            v((8, 128, 1152), BF),
            v((128, 640), BF),
            v((128, 640), BF),
            v((128, 192), BF),
            v((128, 1), F32),
            v((128, 1), F32),
            v((128, 512), F32),
            v((128, 640), F32),
            v((8, 64, 256), BF),
            v((7, 64, 256), BF),
            v((8, 128), F32),
            v((7, 8, 128), F32),
            v((8, 64, 256), BF),
            v((64, 256), F32),
            v((40, 8, 256), BF),
            v((8, 40, 8, 256), BF),
            v((24, 8, 8, 256), BF),
            v((24, 8, 8, 256), BF),
            v((512, 176), F32),
            v((512, 176), F32),
            v((512, 176), BF),
            v((8, 40, 8, 256), BF),
            v((2, 8, 40, 8, 256), BF),
            v((40, 8, 256), BF),
            v((40, 8, 256), BF),
            v((24, 8, 8, 256), BF),
            v((24, 8, 8, 256), BF),
            v((8, 64, 256), BF),
            v((7, 64, 256), BF),
            dma, dma((8,)),
            dma, dma((2,)), dma((3,)), dma((3,)), dma, dma((2, 8)),
            dma, dma, dma, dma, dma, dma,
            dma, dma((2,)), dma, dma, dma, dma((2, 8)),
            dma, dma((2, 2, 8)),
            dma, dma, dma, dma, dma, dma,
        ],
        compiler_params=pltpu.CompilerParams(
            collective_id=0, has_side_effects=True, vmem_limit_bytes=56 * 1024 * 1024
        ),
        name="layer",
    )(
        lengths, query_nope, query_rope, key_absorb, norm_gain, expert_ids.T, block_table, subtree_moves[0].T,
        hidden_in, new_latent, value_absorb, output_proj, router_proj.T,
        latent_cache, expert_gate[0].T, expert_up[0].T, expert_down,
    )


def solution(mesh):
    in_specs = (
        P("ep", None), P("ep", "grp"), P("ep", "grp"), P("ep", None), P("ep", None),
        P("grp", None, None), P("grp", None, None), P("grp", None), P(), P(), P("ep", None),
        P("ep", None, "grp"), P("ep", None, "grp"), P("ep", "grp", None), P("ep", None), P("ep"),
        P("ep", None, None),
    )
    return jax.shard_map(local, mesh=mesh, in_specs=in_specs, out_specs=P("ep", "grp"), check_vma=False)
```

```python
import jax
import jax.numpy as jnp
from jax import lax
from jax.experimental import pallas as pl
from jax.experimental.pallas import tpu as pltpu
from jax.sharding import PartitionSpec as P

BF = jnp.bfloat16
F32 = jnp.float32
MESH = pl.DeviceIdType.MESH
NG = 8
NE = 64
NEG = -1e30


def iota(shape, dim):
    return lax.broadcasted_iota(jnp.int32, shape, dim)


def hot(condition):
    return jnp.where(condition, 1.0, 0.0).astype(BF)


def dot(a, b):
    return jnp.dot(a, b, preferred_element_type=F32)


def dot_nt(a, b):
    return lax.dot_general(a, b, (((1,), (1,)), ((), ())), preferred_element_type=F32)


def dot_tn(a, b):
    return lax.dot_general(a, b, (((0,), (0,)), ((), ())), preferred_element_type=F32)


def await_bytes(ref, sem):
    pltpu.make_async_copy(ref, ref, sem).wait()


def kernel(
    len_ref, qn, qr, ka, gain, ids, bt, mv, hid_hbm, nl_hbm, va_hbm, op_hbm, router_hbm, cache_hbm, wg_hbm, wu_hbm, wd_hbm,
    out,
    hid, nl, va, op, router, wg, wu, wd, msg, far, pool, qe, qo, use, m_ref, l_ref, acc_e, acc_o, p3s, p3r, p4s, p4r, nrm, st, xs, gath, xn, gn,
    acc_g, acc_u, act, part, rsr, ys, ret, yn, rn, mns, mnr, mix_n, mix_f,
    cache_sem, w_sem, e1s, e1r, n1s, n1r, a1s, a1r, p3ss, p3rs, p4ss, p4rs, nxs, nxr, e2s, e2r, n2s, n2r, a2s, a2r, rss, rsrs, e3s, e3r, n3s, n3r, mxs, mxr,
):
    g = lax.axis_index("grp")
    me = lax.axis_index("ep")
    scale = (128 + 64) ** (-0.5)
    sent = []

    def peer(k):
        return lax.rem(g + (k + NG), NG)

    def loop(lo, hi, body):
        def step(i, carry):
            body(i)
            return carry

        lax.fori_loop(lo, hi, step, 0)

    barrier = pltpu.get_barrier_semaphore()
    loop(1, NE, lambda k: pl.semaphore_signal(
        barrier, inc=1, device_id={"ep": lax.rem(me + k, NE)}, device_id_type=MESH))
    loop(1, NG, lambda k: pl.semaphore_signal(barrier, inc=1, device_id={"grp": peer(k)}, device_id_type=MESH))

    cache = pool.at[pl.ds(3, 4)]
    for p in range(8):
        pltpu.make_async_copy(
            cache_hbm.at[:, pl.ds(1152 * p, 1152)], pool.at[3 + p // 2, pl.ds(64 * (p % 2), 64)], cache_sem
        ).start()
    w_copies = [
        pltpu.make_async_copy(wg_hbm, wg, w_sem.at[0]),
        pltpu.make_async_copy(wu_hbm, wu, w_sem.at[1]),
        pltpu.make_async_copy(wd_hbm.at[0], wd, w_sem.at[2]),
    ]
    o_copies = [
        pltpu.make_async_copy(nl_hbm, nl, w_sem.at[3]),
        pltpu.make_async_copy(va_hbm, va, w_sem.at[4]),
        pltpu.make_async_copy(op_hbm, op, w_sem.at[5]),
        pltpu.make_async_copy(hid_hbm, hid, w_sem.at[6]),
        pltpu.make_async_copy(router_hbm, router, w_sem.at[7]),
    ]
    for copy in o_copies:
        copy.start()
    for copy in w_copies:
        copy.start()

    z = (me // 2) % 8
    xc = (me // 16) * 2 + me % 2

    def rank(xc_, z_):
        return (xc_ // 2) * 16 + z_ * 2 + xc_ % 2

    def away(j):
        return jnp.where(j > 4, 2 + j, jnp.where(j % 2 == 0, 2 + j // 2, 6 - j // 2))

    def ahead(j):
        return lax.rem(z + away(j), 8)

    def behind(j):
        return lax.rem(z + 16 - away(j), 8)

    await_bytes(cache, cache_sem)

    def build(k):
        row = iota((128, 64), 0)
        slot_ = row // 16
        to_far = jnp.where(slot_ < 5, rank(lax.rem(g - xc + 8, 8), ahead(slot_)), -1)
        to_near = rank(slot_, lax.rem(z + k + 7, 8))
        sel = hot(iota((128, 64), 1) == jnp.where(k == 3, to_far, to_near))
        picked = dot_nt(sel, mv[...].astype(F32).astype(BF))
        rk = iota((128, 1), 0)
        blk = jnp.where((rk // 8) % 2 == 0, picked[:, 0:1], picked[:, 1:2])
        code = jnp.where(blk < -0.5, -1.0, blk + (64 * (rk % 8)).astype(F32)).astype(jnp.int32)
        big = hot(iota((128, 512), 1) == code)
        msg[k] = dot(big, cache[...].reshape(512, 1152)).astype(BF).reshape(8, 16, 1152)

    build(3)
    pl.semaphore_wait(barrier, NE - 1 + NG - 1)

    loop(0, 5, lambda j: pltpu.make_async_remote_copy(
        msg.at[3, j], far.at[g, pl.ds(pl.multiple_of(16 * j, 16), 16)], e1s, e1r.at[j],
        device_id={"ep": rank(lax.rem(g - xc + 8, 8), ahead(j))}, device_id_type=MESH,
    ).start())
    sent.append(lambda: await_bytes(msg.at[3, pl.ds(0, 5)], e1s))
    loop(0, 3, build)

    def move_near(k):
        def one(j):
            to = rank(j, lax.rem(z + k + 7, 8))
            there = pool.at[k, pl.ds(pl.multiple_of(16 * xc, 16), 16)]

            @pl.when(to == me)
            def _():
                pltpu.make_async_copy(msg.at[k, j], there, n1r.at[k]).start()

            @pl.when(to != me)
            def _():
                pltpu.make_async_remote_copy(
                    msg.at[k, j], there, n1s.at[k], n1r.at[k], device_id={"ep": to}, device_id_type=MESH
                ).start()

        loop(0, 8, one)

    for h in range(2):
        rows = pl.ds(64 * h, 64)
        q_lat = dot(qn[:, 128 * h : 128 * h + 128], ka[h]).astype(BF)
        a, b = iota((128, 128), 0), iota((128, 128), 1)
        rope = dot(qr[...], hot((b < 64) & (a == b + 64 * h))).astype(BF)
        qe[rows, 0:512] = q_lat
        qe[rows, 512:640] = rope
    qo[...] = dot(qe[...], hot(iota((640, 640), 1) == iota((640, 640), 0) + 64)).astype(BF)

    req = iota((16, 64), 0)
    lens = jnp.zeros((16, 64), jnp.int32)
    for i in range(16):
        lens = jnp.where(req == i, len_ref[i], lens)
    count = jnp.clip(lens - 16 * iota((16, 64), 1), 0, 16)
    table = bt[...]
    addr = iota((16, 192), 1)
    usable = jnp.zeros((16, 192), jnp.int32)
    for p in range(64):
        usable = usable + jnp.where(table[:, p : p + 1] == addr, count[:, p : p + 1], 0)
    lam = iota((128, 16), 0)
    spread = hot((lam % 64) // 4 == iota((128, 16), 1))
    use[...] = dot(spread, usable.astype(F32).astype(BF)).astype(BF)

    for copy in o_copies:
        copy.wait()
    pool[7, 0:16] = nl[:, 0:1152]
    pool[7, 16:32] = nl[:, 1152:2304]
    pool[7, 32:128] = jnp.zeros((96, 1152), BF)

    acc_e[...] = jnp.zeros_like(acc_e)
    acc_o[...] = jnp.zeros_like(acc_o)
    m_ref[...] = jnp.full_like(m_ref, NEG)
    l_ref[...] = jnp.zeros_like(l_ref)

    def attend(parts):
        scores = []
        m = m_ref[...]
        m_new = m
        for x, c in parts:
            s_e = jnp.where(c > 0.5, dot_nt(qe[...], x[:, 0:640]) * scale, NEG)
            s_o = jnp.where(c > 1.5, dot_nt(qo[...], x[:, 512:1152]) * scale, NEG)
            m_new = jnp.maximum(m_new, jnp.max(jnp.maximum(s_e, s_o), axis=1, keepdims=True))
            scores.append((s_e, s_o))
        f = jnp.exp(m - m_new)
        l = l_ref[...] * f
        out_e = acc_e[...] * f
        out_o = acc_o[...] * f
        for (x, c), (s_e, s_o) in zip(parts, scores):
            p_e = jnp.where(c > 0.5, jnp.exp(s_e - m_new), 0.0)
            p_o = jnp.where(c > 1.5, jnp.exp(s_o - m_new), 0.0)
            l = l + jnp.sum(p_e + p_o, axis=1, keepdims=True)
            out_e = out_e + dot(p_e.astype(BF), x[:, 0:512])
            out_o = out_o + dot(p_o.astype(BF), x[:, 512:1152])
        m_ref[...] = m_new
        l_ref[...] = l
        acc_e[...] = out_e
        acc_o[...] = out_o

    def far_part(o):
        col = iota((192, 80), 1)
        source = rank(lax.rem(o - xc + 8, 8), behind(col // 16))
        place = hot(iota((192, 80), 0) == 64 + 2 * source + (col // 8) % 2)
        return far[o], dot(use[...], place) - (2 * (iota((128, 80), 1) % 8)).astype(F32)

    def attend_pool(i):
        col = iota((192, 128), 1)
        moved = 64 + 2 * rank(col // 16, lax.rem(z + 9 - i, 8)) + (col // 8) % 2
        place = jnp.where(i < 3, moved, col % 64)
        lam, key = iota((128, 128), 0), iota((128, 128), 1)
        pair = jnp.where(i < 3, key % 8, 2 * (i - 3) + key // 64)
        c = dot(use[...], hot(iota((192, 128), 0) == place)) - (2 * pair).astype(F32)
        fresh = jnp.where(((lam % 64) // 4 == key % 16) & (key < 32), lam % 4 + 1 - 2 * (key // 16), 0)
        attend([(pool[i], jnp.where(i == 7, fresh.astype(F32), c))])

    loop(0, 5, lambda q: attend_pool(7 - q))

    PARTS = 5

    def upward(h):
        return 1 - 2 * (h % 2)

    def ring(at, ssem, rsem):
        def send(o, h, way):
            pltpu.make_async_remote_copy(
                at(o, h), at(o, h), ssem, rsem.at[h, o], device_id={"grp": peer(way)}, device_id_type=MESH
            ).start()

        def own(h):
            send(g, h, 1)
            send(g, h, -1)

        def forward(t, h):
            up = upward(h)
            a, b = peer(-up * t), peer(up * t)
            await_bytes(at(a, h), rsem.at[h, a])

            @pl.when(t < 4)
            def _():
                send(a, h, up)
                await_bytes(at(b, h), rsem.at[h, b])

                @pl.when(t < 3)
                def _():
                    send(b, h, -up)

        return own, forward

    def far_at(o, h):
        return far.at[o, pl.ds(pl.multiple_of(16 * h, 16), 16)]

    own_far, forward_far = ring(far_at, a1s, a1r)

    def start_far(h):
        await_bytes(far_at(g, h), e1r.at[h])
        own_far(h)

    loop(0, PARTS, start_far)
    loop(0, 3, move_near)
    sent.append(lambda: await_bytes(msg.at[0], n1s.at[0]))
    sent.append(lambda: await_bytes(msg.at[1, pl.ds(0, 7)], n1s.at[1]))
    sent.append(lambda: await_bytes(msg.at[2], n1s.at[2]))
    attend([far_part(g)])

    def near_chunk(k):
        await_bytes(pool.at[k], n1r.at[k])
        attend_pool(k)

    def step_far(t):
        loop(0, PARTS, lambda h: forward_far(t, h))

        @pl.when(t < 4)
        def _():
            attend([far_part(peer(-t)), far_part(peer(t))])

        @pl.when(t == 3)
        def _():
            loop(0, 3, near_chunk)

    loop(1, 5, step_far)
    attend([far_part(peer(4))])
    sent.append(lambda: await_bytes(far.at[pl.ds(0, 7)], a1s))
    total = acc_e[...] + acc_o[...][:, 64:576]
    latent = (total / l_ref[...]).astype(BF)
    heads = [dot(latent[64 * h : 64 * h + 64], va[h]).astype(BF) for h in range(2)]
    head_out = jnp.concatenate(heads, axis=1)

    def attn_block(k):
        c = peer(k)
        p3s[c] = dot(head_out, op[:, pl.ds(pl.multiple_of(c * 256, 256), 256)]).astype(BF)

        @pl.when(k > 0)
        def _():
            pltpu.make_async_remote_copy(
                p3s.at[c], p3r.at[k - 1], p3ss, p3rs, device_id={"grp": c}, device_id_type=MESH
            ).start()

    loop(0, NG, lambda k: attn_block(NG - 1 - k))
    sent.append(lambda: await_bytes(p3s.at[pl.ds(0, 7)], p3ss))

    def exchange(src, dst, ssem, rsem):
        loop(1, NG, lambda k: pltpu.make_async_remote_copy(
            src(peer(k)), dst.at[k - 1], ssem, rsem, device_id={"grp": peer(k)}, device_id_type=MESH
        ).start())

    ids_v = ids[...]
    expert = iota((64, 64), 0)
    named_t = jnp.zeros((64, 64), F32)
    for k in range(6):
        named_t = named_t + jnp.where(ids_v[k : k + 1, :] == expert, 1.0, 0.0)
    identity = hot(iota((64, 64), 0) == iota((64, 64), 1))
    named_b = dot_nt(identity, named_t.astype(BF)).astype(BF)
    before = dot(hot(iota((64, 64), 1) < iota((64, 64), 0)), named_b).astype(BF)
    def choose(first, slots):
        col = iota((64, 8 * slots), 1)
        n = first + col // 8
        widen = hot(iota((64, 8 * slots), 0) == rank(n % 8, ahead(n // 8)))
        at_slot = jnp.abs(dot(before, widen) - (col % 8).astype(F32)) < 0.5
        return widen, hot((dot(named_b, widen) > 0.5) & at_slot)

    widen_far, chosen_far = choose(0, 40)
    widen_near, chosen_near = choose(40, 24)

    await_bytes(p3r, p3rs)
    cols = pl.ds(pl.multiple_of(g * 256, 256), 256)
    attn = p3s[g].astype(F32)
    for k in range(NG - 1):
        attn = attn + p3r[k].astype(F32)
    state = hid[:, cols].astype(F32) + attn
    st[...] = state
    square = jnp.sum(state * state, axis=1, keepdims=True)
    diagonal = iota((64, 128), 0) == iota((64, 128), 1)
    p4s[...] = jnp.broadcast_to(jnp.sum(jnp.where(diagonal, square, 0.0), axis=0, keepdims=True), (8, 128))
    exchange(lambda c: p4s, p4r, p4ss, p4rs)
    sent.append(lambda: await_bytes(p4r, p4ss))
    await_bytes(p4r, p4rs)
    squares = p4s[...]
    for k in range(NG - 1):
        squares = squares + p4r[k]
    square = jnp.sum(jnp.where(diagonal, squares[0:1], 0.0), axis=1, keepdims=True)
    inverse = lax.rsqrt(square / 2048.0 + 1e-06)
    gains = gain[...].astype(F32).reshape(16, 128)
    row = iota((16, 128), 0)
    gain_cols = jnp.concatenate(
        [jnp.sum(jnp.where(row == 2 * g + i, gains, 0.0), axis=0, keepdims=True) for i in range(2)], axis=1
    )
    normed = (state * inverse * gain_cols).astype(BF)

    nrm[g] = normed
    loop(1, NG, lambda k: pltpu.make_async_remote_copy(
        nrm.at[g], nrm.at[g], nxs, nxr, device_id={"grp": peer(k)}, device_id_type=MESH
    ).start())
    sent.append(lambda: await_bytes(nrm.at[pl.ds(0, 7)], nxs))

    xs[...] = dot_tn(chosen_far, normed).reshape(40, 8, 256).astype(BF)

    def dispatch(n):
        xt = lax.rem(n + xc, 8)
        pltpu.make_async_remote_copy(
            xs.at[8 * (n // 8) + xt], gath.at[g, 8 * (n // 8) + xc], e2s, e2r.at[n // 8],
            device_id={"ep": rank(xt, ahead(n // 8))}, device_id_type=MESH,
        ).start()

    loop(0, 40, dispatch)
    sent.append(lambda: await_bytes(xs, e2s))

    def dispatch_near():
        await_bytes(nrm.at[pl.ds(0, 7)], nxr)
        for j in range(3):
            _, chosen_j = choose(40 + 8 * j, 8)

            def block(o):
                xn[8 * j : 8 * j + 8, o] = dot_tn(chosen_j, nrm[o]).reshape(8, 8, 256).astype(BF)

            loop(0, 8, block)

            def one(n):
                xt = lax.rem(n + xc, 8)
                to = rank(xt, lax.rem(z + 7 + j, 8))
                here, there = xn.at[8 * j + xt], gn.at[8 * j + xc]

                @pl.when(to == me)
                def _():
                    pltpu.make_async_copy(here, there, n2r).start()

                @pl.when(to != me)
                def _():
                    pltpu.make_async_remote_copy(
                        here, there, n2s, n2r, device_id={"ep": to}, device_id_type=MESH
                    ).start()

            loop(0, 8, one)
        sent.append(lambda: await_bytes(xn.at[pl.ds(0, 23)], n2s))

    def gates():
        logits = jnp.zeros((64, 64), F32)
        for o in range(8):
            logits = logits + dot_nt(nrm[o], router[:, 256 * o : 256 * o + 256])
        weight = jnp.where(named_b.astype(F32) > 0.5, jax.nn.sigmoid(logits), 0.0)
        weight = weight / jnp.sum(weight, axis=1, keepdims=True)
        w_hi = weight.astype(BF)
        w_lo = (weight - w_hi.astype(F32)).astype(BF)
        for mix, widen, chosen in ((mix_n, widen_near, chosen_near), (mix_f, widen_far, chosen_far)):
            mask = chosen.astype(F32)
            mix[0] = (dot(w_hi, widen) * mask).astype(BF)
            mix[1] = (dot(w_lo, widen) * mask).astype(BF)

    for copy in w_copies:
        copy.wait()
    acc_g[...] = jnp.zeros_like(acc_g)
    acc_u[...] = jnp.zeros_like(acc_u)

    def part_of(h):
        return pl.ds(8 * h, 8)

    def gath_at(o, h):
        return gath.at[o, part_of(h)]

    far_rows, near_rows = pl.ds(0, 320), pl.ds(320, 192)

    def add_columns(x, o, rows):
        lanes = pl.ds(pl.multiple_of(o * 256, 256), 256)
        acc_g[rows, :] += dot_nt(x, wg[:, lanes])
        acc_u[rows, :] += dot_nt(x, wu[:, lanes])

    def expert_columns(o):
        add_columns(gath[o].reshape(320, 256), o, far_rows)

    def activate(rows):
        gate = acc_g[rows, :]
        act[rows, :] = (gate / (1.0 + jnp.exp(-gate)) * acc_u[rows, :]).astype(BF)

    def pass_on(c, h, way):
        d = (1 - way) // 2
        pltpu.make_async_remote_copy(
            part.at[c, part_of(h)], rsr.at[d, c, part_of(h)], rss, rsrs.at[d, h, c],
            device_id={"grp": peer(way)}, device_id_type=MESH,
        ).start()

    def down_block(i):
        near = 4 - (i + 1) // 2
        way = 1 - 2 * ((i + 1) % 2)
        c = peer(way * near)
        lanes = pl.ds(pl.multiple_of(c * 256, 256), 256)
        part[c] = dot(act[far_rows, :], wd[:, lanes]).reshape(40, 8, 256).astype(BF)

        @pl.when(i == 0)
        def _():
            loop(0, PARTS, lambda h: pass_on(c, PARTS - 1 - h, upward(h)))

        @pl.when((i == 1) | (i == 2))
        def _():
            def one(h):
                @pl.when(upward(h) != way)
                def _():
                    pass_on(c, h, way)

            loop(0, PARTS, lambda h: one(PARTS - 1 - h))

    def add_on(t, h):
        up = upward(h)

        def stream(i):
            way = up * (1 - 2 * i)
            c = peer(way * (4 - i - t))
            d = (1 - way) // 2
            await_bytes(rsr.at[d, c, part_of(h)], rsrs.at[d, h, c])
            part[c, part_of(h)] = (part[c, part_of(h)].astype(F32) + rsr[d, c, part_of(h)].astype(F32)).astype(BF)
            pass_on(c, h, way)

        loop(0, jnp.where(t < 3, 2, 1), stream)

    def finish(h):
        total_h = part[g, part_of(h)].astype(F32)
        for d in range(2):
            await_bytes(rsr.at[d, g, part_of(h)], rsrs.at[d, h, g])
            total_h = total_h + rsr[d, g, part_of(h)].astype(F32)
        ys[part_of(h)] = total_h.astype(BF)
        loop(8 * h, 8 * h + 8, give_back)

    def give_back(n):
        xt = lax.rem(n + xc, 8)
        pltpu.make_async_remote_copy(
            ys.at[8 * (n // 8) + xt], ret.at[8 * (n // 8) + xc], e3s, e3r,
            device_id={"ep": rank(xt, behind(n // 8))}, device_id_type=MESH,
        ).start()

    def give_back_near(n):
        xt = lax.rem(n + xc, 8)
        to = rank(xt, lax.rem(z + 9 - n // 8, 8))
        here, there = yn.at[8 * (n // 8) + xt], rn.at[8 * (n // 8) + xc]

        @pl.when(to == me)
        def _():
            pltpu.make_async_copy(here, there, n3r).start()

        @pl.when(to != me)
        def _():
            pltpu.make_async_remote_copy(here, there, n3s, n3r, device_id={"ep": to}, device_id_type=MESH).start()

    own_rows, forward_rows = ring(gath_at, a2s, a2r)

    def start_rows(h):
        await_bytes(gath_at(g, h), e2r.at[h])
        own_rows(h)

    loop(0, PARTS, start_rows)
    dispatch_near()
    expert_columns(g)

    def step_expert(t):
        loop(0, PARTS, lambda h: forward_rows(t, h))
        loop(0, jnp.where(t < 4, 2, 1), lambda i: expert_columns(peer(t * (2 * i - 1))))

        @pl.when(t == 1)
        def _():
            gates()

        @pl.when(t == 3)
        def _():
            await_bytes(gn, n2r)
            loop(0, 8, lambda o: add_columns(gn[:, o].reshape(192, 256), o, near_rows))
            activate(near_rows)

    loop(1, 5, step_expert)
    sent.append(lambda: await_bytes(gath.at[pl.ds(0, 7)], a2s))
    activate(far_rows)
    loop(0, 5, down_block)

    def near_block(c):
        lanes = pl.ds(pl.multiple_of(c * 256, 256), 256)
        yn[:, c] = dot(act[near_rows, :], wd[:, lanes]).reshape(24, 8, 256).astype(BF)

    def mix_block(k):
        c = peer(k)
        results = rn[:, c].reshape(192, 256)
        mns[c] = (dot(mix_n[0], results) + dot(mix_n[1], results)).astype(BF)

        @pl.when(k > 0)
        def _():
            pltpu.make_async_remote_copy(
                mns.at[c], mnr.at[k - 1], mxs, mxr, device_id={"grp": c}, device_id_type=MESH
            ).start()

    loop(0, 8, near_block)
    loop(0, 24, give_back_near)

    def step_sum(t):
        loop(0, PARTS, lambda h: add_on(t, PARTS - 1 - h))

        @pl.when(t == 1)
        def _():
            loop(5, 8, down_block)

    loop(1, 4, step_sum)
    await_bytes(rn, n3r)
    loop(0, NG, lambda k: mix_block(NG - 1 - k))
    sent.append(lambda: await_bytes(mnr, mxs))
    sent.append(lambda: await_bytes(yn.at[pl.ds(0, 23)], n3s))
    loop(0, PARTS, lambda h: finish(PARTS - 1 - h))
    sent.append(lambda: await_bytes(part.at[pl.ds(0, 7)], rss))
    sent.append(lambda: await_bytes(ys, e3s))

    await_bytes(ret, e3r)
    results = ret[...].reshape(320, 256)
    total = st[...] + dot(mix_f[0], results) + dot(mix_f[1], results) + mns[g].astype(F32)
    await_bytes(mnr, mxr)
    for k in range(NG - 1):
        total = total + mnr[k].astype(F32)
    out[...] = total.astype(BF)

    for wait in sent:
        wait()


def local(
    hidden_in, query_nope, query_rope, new_latent, latent_cache, key_absorb, value_absorb, output_proj, norm_gain,
    router_proj, expert_ids, expert_gate, expert_up, expert_down, block_table, lengths, subtree_moves,
):
    vmem = pl.BlockSpec(memory_space=pltpu.VMEM)
    anywhere = pl.BlockSpec(memory_space=pl.ANY)
    dma = pltpu.SemaphoreType.DMA
    v = pltpu.VMEM
    return pl.pallas_call(
        kernel,
        out_shape=jax.ShapeDtypeStruct((64, 256), BF),
        in_specs=[pl.BlockSpec(memory_space=pltpu.SMEM)] + [vmem] * 7 + [anywhere] * 9,
        out_specs=vmem,
        scratch_shapes=[
            v((64, 2048), BF),
            v((16, 2304), BF),
            v((2, 512, 128), BF),
            v((256, 2048), BF),
            v((64, 2048), BF),
            v((176, 2048), BF),
            v((176, 2048), BF),
            v((176, 2048), BF),
            v((4, 8, 16, 1152), BF),
            v((8, 80, 1152), BF),
            v((8, 128, 1152), BF),
            v((128, 640), BF),
            v((128, 640), BF),
            v((128, 192), BF),
            v((128, 1), F32),
            v((128, 1), F32),
            v((128, 512), F32),
            v((128, 640), F32),
            v((8, 64, 256), BF),
            v((7, 64, 256), BF),
            v((8, 128), F32),
            v((7, 8, 128), F32),
            v((8, 64, 256), BF),
            v((64, 256), F32),
            v((40, 8, 256), BF),
            v((8, 40, 8, 256), BF),
            v((24, 8, 8, 256), BF),
            v((24, 8, 8, 256), BF),
            v((512, 176), F32),
            v((512, 176), F32),
            v((512, 176), BF),
            v((8, 40, 8, 256), BF),
            v((2, 8, 40, 8, 256), BF),
            v((40, 8, 256), BF),
            v((40, 8, 256), BF),
            v((24, 8, 8, 256), BF),
            v((24, 8, 8, 256), BF),
            v((8, 64, 256), BF),
            v((7, 64, 256), BF),
            v((2, 64, 192), BF),
            v((2, 64, 320), BF),
            dma, dma((8,)),
            dma, dma((5,)), dma((3,)), dma((3,)), dma, dma((5, 8)),
            dma, dma, dma, dma, dma, dma,
            dma, dma((5,)), dma, dma, dma, dma((5, 8)),
            dma, dma((2, 5, 8)),
            dma, dma, dma, dma, dma, dma,
        ],
        compiler_params=pltpu.CompilerParams(
            collective_id=0, has_side_effects=True, vmem_limit_bytes=56 * 1024 * 1024
        ),
        name="layer",
    )(
        lengths, query_nope, query_rope, key_absorb, norm_gain, expert_ids.T, block_table, subtree_moves[0].T,
        hidden_in, new_latent, value_absorb, output_proj, router_proj.T,
        latent_cache, expert_gate[0].T, expert_up[0].T, expert_down,
    )


def solution(mesh):
    in_specs = (
        P("ep", None), P("ep", "grp"), P("ep", "grp"), P("ep", None), P("ep", None),
        P("grp", None, None), P("grp", None, None), P("grp", None), P(), P(), P("ep", None),
        P("ep", None, "grp"), P("ep", None, "grp"), P("ep", "grp", None), P("ep", None), P("ep"),
        P("ep", None, None),
    )
    return jax.shard_map(local, mesh=mesh, in_specs=in_specs, out_specs=P("ep", "grp"), check_vma=False)
```

```python
import jax
import jax.numpy as jnp
from jax import lax
from jax.experimental import pallas as pl
from jax.experimental.pallas import tpu as pltpu
from jax.sharding import PartitionSpec as P

BF = jnp.bfloat16
F32 = jnp.float32
MESH = pl.DeviceIdType.MESH
NG = 8
NE = 64
NEG = -1e30


def iota(shape, dim):
    return lax.broadcasted_iota(jnp.int32, shape, dim)


def hot(condition):
    return jnp.where(condition, 1.0, 0.0).astype(BF)


def dot(a, b):
    return jnp.dot(a, b, preferred_element_type=F32)


def dot_nt(a, b):
    return lax.dot_general(a, b, (((1,), (1,)), ((), ())), preferred_element_type=F32)


def dot_tn(a, b):
    return lax.dot_general(a, b, (((0,), (0,)), ((), ())), preferred_element_type=F32)


def await_bytes(ref, sem):
    pltpu.make_async_copy(ref, ref, sem).wait()


def kernel(
    len_ref, qn, qr, ka, gain, ids, bt, mv, hid_hbm, nl_hbm, va_hbm, op_hbm, router_hbm, cache_hbm, wg_hbm, wu_hbm, wd_hbm,
    out,
    hid, nl, va, op, router, wg, wu, wd, msg, far, pool, qe, qo, use, m_ref, l_ref, acc_e, acc_o, p3s, p3r, p4s, p4r, nrm, st, xs, gath, xn, gn,
    acc_g, acc_u, act, part, rsr, ys, ret, yn, rn, mns, mnr, mix_n, mix_f,
    cache_sem, w_sem, e1s, e1r, n1s, n1r, a1s, a1r, p3ss, p3rs, p4ss, p4rs, nxs, nxr, e2s, e2r, n2s, n2r, a2s, a2r, rss, rsrs, e3s, e3r, n3s, n3r, mxs, mxr,
):
    g = lax.axis_index("grp")
    me = lax.axis_index("ep")
    scale = (128 + 64) ** (-0.5)
    sent = []

    def peer(k):
        return lax.rem(g + (k + NG), NG)

    def farthest(i):
        return jnp.where(i % 2 == 1, 4 - (i + 1) // 2, 4 + i // 2)

    def loop(lo, hi, body):
        def step(i, carry):
            body(i)
            return carry

        lax.fori_loop(lo, hi, step, 0)

    barrier = pltpu.get_barrier_semaphore()
    loop(1, NE, lambda k: pl.semaphore_signal(
        barrier, inc=1, device_id={"ep": lax.rem(me + k, NE)}, device_id_type=MESH))
    loop(1, NG, lambda k: pl.semaphore_signal(barrier, inc=1, device_id={"grp": peer(k)}, device_id_type=MESH))

    cache = pool.at[pl.ds(3, 4)]
    for p in range(8):
        pltpu.make_async_copy(
            cache_hbm.at[:, pl.ds(1152 * p, 1152)], pool.at[3 + p // 2, pl.ds(64 * (p % 2), 64)], cache_sem
        ).start()
    w_copies = [
        pltpu.make_async_copy(wg_hbm, wg, w_sem.at[0]),
        pltpu.make_async_copy(wu_hbm, wu, w_sem.at[1]),
        pltpu.make_async_copy(wd_hbm.at[0], wd, w_sem.at[2]),
    ]
    o_copies = [
        pltpu.make_async_copy(nl_hbm, nl, w_sem.at[3]),
        pltpu.make_async_copy(va_hbm, va, w_sem.at[4]),
        pltpu.make_async_copy(op_hbm, op, w_sem.at[5]),
        pltpu.make_async_copy(hid_hbm, hid, w_sem.at[6]),
        pltpu.make_async_copy(router_hbm, router, w_sem.at[7]),
    ]
    for copy in o_copies:
        copy.start()
    for copy in w_copies:
        copy.start()

    z = (me // 2) % 8
    xc = (me // 16) * 2 + me % 2

    def rank(xc_, z_):
        return (xc_ // 2) * 16 + z_ * 2 + xc_ % 2

    def away(j):
        return jnp.where(j > 4, 2 + j, jnp.where(j % 2 == 0, 2 + j // 2, 6 - j // 2))

    def ahead(j):
        return lax.rem(z + away(j), 8)

    def behind(j):
        return lax.rem(z + 16 - away(j), 8)

    await_bytes(cache, cache_sem)

    def build(k):
        row = iota((128, 64), 0)
        slot_ = row // 16
        to_far = jnp.where(slot_ < 5, rank(lax.rem(g - xc + 8, 8), ahead(slot_)), -1)
        to_near = rank(slot_, lax.rem(z + k + 7, 8))
        sel = hot(iota((128, 64), 1) == jnp.where(k == 3, to_far, to_near))
        picked = dot_nt(sel, mv[...].astype(F32).astype(BF))
        rk = iota((128, 1), 0)
        blk = jnp.where((rk // 8) % 2 == 0, picked[:, 0:1], picked[:, 1:2])
        code = jnp.where(blk < -0.5, -1.0, blk + (64 * (rk % 8)).astype(F32)).astype(jnp.int32)
        big = hot(iota((128, 512), 1) == code)
        msg[k] = dot(big, cache[...].reshape(512, 1152)).astype(BF).reshape(8, 16, 1152)

    build(3)
    pl.semaphore_wait(barrier, NE - 1 + NG - 1)

    loop(0, 5, lambda j: pltpu.make_async_remote_copy(
        msg.at[3, j], far.at[g, pl.ds(pl.multiple_of(16 * j, 16), 16)], e1s, e1r.at[j],
        device_id={"ep": rank(lax.rem(g - xc + 8, 8), ahead(j))}, device_id_type=MESH,
    ).start())
    sent.append(lambda: await_bytes(msg.at[3, pl.ds(0, 5)], e1s))
    loop(0, 3, build)

    def move_near(k):
        def one(j):
            to = rank(j, lax.rem(z + k + 7, 8))
            there = pool.at[k, pl.ds(pl.multiple_of(16 * xc, 16), 16)]

            @pl.when(to == me)
            def _():
                pltpu.make_async_copy(msg.at[k, j], there, n1r.at[k]).start()

            @pl.when(to != me)
            def _():
                pltpu.make_async_remote_copy(
                    msg.at[k, j], there, n1s.at[k], n1r.at[k], device_id={"ep": to}, device_id_type=MESH
                ).start()

        loop(0, 8, one)

    for h in range(2):
        rows = pl.ds(64 * h, 64)
        q_lat = dot(qn[:, 128 * h : 128 * h + 128], ka[h]).astype(BF)
        a, b = iota((128, 128), 0), iota((128, 128), 1)
        rope = dot(qr[...], hot((b < 64) & (a == b + 64 * h))).astype(BF)
        qe[rows, 0:512] = q_lat
        qe[rows, 512:640] = rope
    qo[...] = dot(qe[...], hot(iota((640, 640), 1) == iota((640, 640), 0) + 64)).astype(BF)

    req = iota((16, 64), 0)
    lens = jnp.zeros((16, 64), jnp.int32)
    for i in range(16):
        lens = jnp.where(req == i, len_ref[i], lens)
    count = jnp.clip(lens - 16 * iota((16, 64), 1), 0, 16)
    table = bt[...]
    addr = iota((16, 192), 1)
    usable = jnp.zeros((16, 192), jnp.int32)
    for p in range(64):
        usable = usable + jnp.where(table[:, p : p + 1] == addr, count[:, p : p + 1], 0)
    lam = iota((128, 16), 0)
    spread = hot((lam % 64) // 4 == iota((128, 16), 1))
    use[...] = dot(spread, usable.astype(F32).astype(BF)).astype(BF)

    for copy in o_copies:
        copy.wait()
    pool[7, 0:16] = nl[:, 0:1152]
    pool[7, 16:32] = nl[:, 1152:2304]
    pool[7, 32:128] = jnp.zeros((96, 1152), BF)

    acc_e[...] = jnp.zeros_like(acc_e)
    acc_o[...] = jnp.zeros_like(acc_o)
    m_ref[...] = jnp.full_like(m_ref, NEG)
    l_ref[...] = jnp.zeros_like(l_ref)

    def attend(parts):
        scores = []
        m = m_ref[...]
        m_new = m
        for x, c in parts:
            s_e = jnp.where(c > 0.5, dot_nt(qe[...], x[:, 0:640]) * scale, NEG)
            s_o = jnp.where(c > 1.5, dot_nt(qo[...], x[:, 512:1152]) * scale, NEG)
            m_new = jnp.maximum(m_new, jnp.max(jnp.maximum(s_e, s_o), axis=1, keepdims=True))
            scores.append((s_e, s_o))
        f = jnp.exp(m - m_new)
        l = l_ref[...] * f
        out_e = acc_e[...] * f
        out_o = acc_o[...] * f
        for (x, c), (s_e, s_o) in zip(parts, scores):
            p_e = jnp.where(c > 0.5, jnp.exp(s_e - m_new), 0.0)
            p_o = jnp.where(c > 1.5, jnp.exp(s_o - m_new), 0.0)
            l = l + jnp.sum(p_e + p_o, axis=1, keepdims=True)
            out_e = out_e + dot(p_e.astype(BF), x[:, 0:512])
            out_o = out_o + dot(p_o.astype(BF), x[:, 512:1152])
        m_ref[...] = m_new
        l_ref[...] = l
        acc_e[...] = out_e
        acc_o[...] = out_o

    def far_part(o):
        col = iota((192, 80), 1)
        source = rank(lax.rem(o - xc + 8, 8), behind(col // 16))
        place = hot(iota((192, 80), 0) == 64 + 2 * source + (col // 8) % 2)
        return far[o], dot(use[...], place) - (2 * (iota((128, 80), 1) % 8)).astype(F32)

    def attend_pool(i):
        col = iota((192, 128), 1)
        moved = 64 + 2 * rank(col // 16, lax.rem(z + 9 - i, 8)) + (col // 8) % 2
        place = jnp.where(i < 3, moved, col % 64)
        lam, key = iota((128, 128), 0), iota((128, 128), 1)
        pair = jnp.where(i < 3, key % 8, 2 * (i - 3) + key // 64)
        c = dot(use[...], hot(iota((192, 128), 0) == place)) - (2 * pair).astype(F32)
        fresh = jnp.where(((lam % 64) // 4 == key % 16) & (key < 32), lam % 4 + 1 - 2 * (key // 16), 0)
        attend([(pool[i], jnp.where(i == 7, fresh.astype(F32), c))])

    loop(0, 5, lambda q: attend_pool(7 - q))

    PARTS = 5

    def upward(h):
        return 1 - 2 * (h % 2)

    def ring(at, ssem, rsem):
        def send(o, h, way):
            pltpu.make_async_remote_copy(
                at(o, h), at(o, h), ssem, rsem.at[h, o], device_id={"grp": peer(way)}, device_id_type=MESH
            ).start()

        def own(h):
            send(g, h, 1)
            send(g, h, -1)

        def forward(t, h):
            up = upward(h)
            a, b = peer(-up * t), peer(up * t)
            await_bytes(at(a, h), rsem.at[h, a])

            @pl.when(t < 4)
            def _():
                send(a, h, up)
                await_bytes(at(b, h), rsem.at[h, b])

                @pl.when(t < 3)
                def _():
                    send(b, h, -up)

        return own, forward

    def far_at(o, h):
        return far.at[o, pl.ds(pl.multiple_of(16 * h, 16), 16)]

    own_far, forward_far = ring(far_at, a1s, a1r)

    def start_far(h):
        await_bytes(far_at(g, h), e1r.at[h])
        own_far(h)

    loop(0, PARTS, start_far)
    loop(0, 3, move_near)
    sent.append(lambda: await_bytes(msg.at[0], n1s.at[0]))
    sent.append(lambda: await_bytes(msg.at[1, pl.ds(0, 7)], n1s.at[1]))
    sent.append(lambda: await_bytes(msg.at[2], n1s.at[2]))
    attend([far_part(g)])

    def near_chunk(k):
        await_bytes(pool.at[k], n1r.at[k])
        attend_pool(k)

    def step_far(t):
        loop(0, PARTS, lambda h: forward_far(t, h))

        @pl.when(t < 4)
        def _():
            attend([far_part(peer(-t)), far_part(peer(t))])

        @pl.when(t == 3)
        def _():
            loop(0, 3, near_chunk)

    loop(1, 5, step_far)
    attend([far_part(peer(4))])
    sent.append(lambda: await_bytes(far.at[pl.ds(0, 7)], a1s))
    total = acc_e[...] + acc_o[...][:, 64:576]
    latent = (total / l_ref[...]).astype(BF)
    heads = [dot(latent[64 * h : 64 * h + 64], va[h]).astype(BF) for h in range(2)]
    head_out = jnp.concatenate(heads, axis=1)

    def attn_block(k):
        c = peer(k)
        p3s[c] = dot(head_out, op[:, pl.ds(pl.multiple_of(c * 256, 256), 256)]).astype(BF)

        @pl.when(k > 0)
        def _():
            pltpu.make_async_remote_copy(
                p3s.at[c], p3r.at[k - 1], p3ss, p3rs, device_id={"grp": c}, device_id_type=MESH
            ).start()

    loop(0, NG, lambda i: attn_block(farthest(i)))
    sent.append(lambda: await_bytes(p3s.at[pl.ds(0, 7)], p3ss))

    def exchange(src, dst, ssem, rsem):
        loop(1, NG, lambda k: pltpu.make_async_remote_copy(
            src(peer(k)), dst.at[k - 1], ssem, rsem, device_id={"grp": peer(k)}, device_id_type=MESH
        ).start())

    ids_v = ids[...]
    expert = iota((64, 64), 0)
    named_t = jnp.zeros((64, 64), F32)
    for k in range(6):
        named_t = named_t + jnp.where(ids_v[k : k + 1, :] == expert, 1.0, 0.0)
    identity = hot(iota((64, 64), 0) == iota((64, 64), 1))
    named_b = dot_nt(identity, named_t.astype(BF)).astype(BF)
    before = dot(hot(iota((64, 64), 1) < iota((64, 64), 0)), named_b).astype(BF)
    def choose(first, slots):
        col = iota((64, 8 * slots), 1)
        n = first + col // 8
        widen = hot(iota((64, 8 * slots), 0) == rank(n % 8, ahead(n // 8)))
        at_slot = jnp.abs(dot(before, widen) - (col % 8).astype(F32)) < 0.5
        return widen, hot((dot(named_b, widen) > 0.5) & at_slot)

    widen_far, chosen_far = choose(0, 40)
    widen_near, chosen_near = choose(40, 24)

    await_bytes(p3r, p3rs)
    cols = pl.ds(pl.multiple_of(g * 256, 256), 256)
    attn = p3s[g].astype(F32)
    for k in range(NG - 1):
        attn = attn + p3r[k].astype(F32)
    state = hid[:, cols].astype(F32) + attn
    st[...] = state
    square = jnp.sum(state * state, axis=1, keepdims=True)
    diagonal = iota((64, 128), 0) == iota((64, 128), 1)
    p4s[...] = jnp.broadcast_to(jnp.sum(jnp.where(diagonal, square, 0.0), axis=0, keepdims=True), (8, 128))
    exchange(lambda c: p4s, p4r, p4ss, p4rs)
    sent.append(lambda: await_bytes(p4r, p4ss))
    await_bytes(p4r, p4rs)
    squares = p4s[...]
    for k in range(NG - 1):
        squares = squares + p4r[k]
    square = jnp.sum(jnp.where(diagonal, squares[0:1], 0.0), axis=1, keepdims=True)
    inverse = lax.rsqrt(square / 2048.0 + 1e-06)
    gains = gain[...].astype(F32).reshape(16, 128)
    row = iota((16, 128), 0)
    gain_cols = jnp.concatenate(
        [jnp.sum(jnp.where(row == 2 * g + i, gains, 0.0), axis=0, keepdims=True) for i in range(2)], axis=1
    )
    normed = (state * inverse * gain_cols).astype(BF)

    nrm[g] = normed
    loop(0, NG - 1, lambda i: pltpu.make_async_remote_copy(
        nrm.at[g], nrm.at[g], nxs, nxr, device_id={"grp": peer(farthest(i))}, device_id_type=MESH
    ).start())
    sent.append(lambda: await_bytes(nrm.at[pl.ds(0, 7)], nxs))

    xs[...] = dot_tn(chosen_far, normed).reshape(40, 8, 256).astype(BF)

    def dispatch(n):
        xt = lax.rem(n + xc, 8)
        pltpu.make_async_remote_copy(
            xs.at[8 * (n // 8) + xt], gath.at[g, 8 * (n // 8) + xc], e2s, e2r.at[n // 8],
            device_id={"ep": rank(xt, ahead(n // 8))}, device_id_type=MESH,
        ).start()

    loop(0, 40, dispatch)
    sent.append(lambda: await_bytes(xs, e2s))

    def dispatch_near():
        await_bytes(nrm.at[pl.ds(0, 7)], nxr)
        for j in range(3):
            _, chosen_j = choose(40 + 8 * j, 8)

            def block(o):
                xn[8 * j : 8 * j + 8, o] = dot_tn(chosen_j, nrm[o]).reshape(8, 8, 256).astype(BF)

            loop(0, 8, block)

            def one(n):
                xt = lax.rem(n + xc, 8)
                to = rank(xt, lax.rem(z + 7 + j, 8))
                here, there = xn.at[8 * j + xt], gn.at[8 * j + xc]

                @pl.when(to == me)
                def _():
                    pltpu.make_async_copy(here, there, n2r).start()

                @pl.when(to != me)
                def _():
                    pltpu.make_async_remote_copy(
                        here, there, n2s, n2r, device_id={"ep": to}, device_id_type=MESH
                    ).start()

            loop(0, 8, one)
        sent.append(lambda: await_bytes(xn.at[pl.ds(0, 23)], n2s))

    def gates():
        logits = jnp.zeros((64, 64), F32)
        for o in range(8):
            logits = logits + dot_nt(nrm[o], router[:, 256 * o : 256 * o + 256])
        weight = jnp.where(named_b.astype(F32) > 0.5, jax.nn.sigmoid(logits), 0.0)
        weight = weight / jnp.sum(weight, axis=1, keepdims=True)
        w_hi = weight.astype(BF)
        w_lo = (weight - w_hi.astype(F32)).astype(BF)
        for mix, widen, chosen in ((mix_n, widen_near, chosen_near), (mix_f, widen_far, chosen_far)):
            mask = chosen.astype(F32)
            mix[0] = (dot(w_hi, widen) * mask).astype(BF)
            mix[1] = (dot(w_lo, widen) * mask).astype(BF)

    for copy in w_copies:
        copy.wait()
    acc_g[...] = jnp.zeros_like(acc_g)
    acc_u[...] = jnp.zeros_like(acc_u)

    def part_of(h):
        return pl.ds(8 * h, 8)

    def gath_at(o, h):
        return gath.at[o, part_of(h)]

    far_rows, near_rows = pl.ds(0, 320), pl.ds(320, 192)

    def add_columns(x, o, rows):
        lanes = pl.ds(pl.multiple_of(o * 256, 256), 256)
        acc_g[rows, :] += dot_nt(x, wg[:, lanes])
        acc_u[rows, :] += dot_nt(x, wu[:, lanes])

    def expert_columns(o):
        add_columns(gath[o].reshape(320, 256), o, far_rows)

    def activate(rows):
        gate = acc_g[rows, :]
        act[rows, :] = (gate / (1.0 + jnp.exp(-gate)) * acc_u[rows, :]).astype(BF)

    def pass_on(c, h, way):
        d = (1 - way) // 2
        pltpu.make_async_remote_copy(
            part.at[c, part_of(h)], rsr.at[d, c, part_of(h)], rss, rsrs.at[d, h, c],
            device_id={"grp": peer(way)}, device_id_type=MESH,
        ).start()

    def down_block(i):
        near = 4 - (i + 1) // 2
        way = 1 - 2 * ((i + 1) % 2)
        c = peer(way * near)
        lanes = pl.ds(pl.multiple_of(c * 256, 256), 256)
        part[c] = dot(act[far_rows, :], wd[:, lanes]).reshape(40, 8, 256).astype(BF)

        @pl.when(i == 0)
        def _():
            loop(0, PARTS, lambda h: pass_on(c, PARTS - 1 - h, upward(h)))

        @pl.when((i == 1) | (i == 2))
        def _():
            def one(h):
                @pl.when(upward(h) != way)
                def _():
                    pass_on(c, h, way)

            loop(0, PARTS, lambda h: one(PARTS - 1 - h))

    def add_on(t, h):
        up = upward(h)

        def stream(i):
            way = up * (1 - 2 * i)
            c = peer(way * (4 - i - t))
            d = (1 - way) // 2
            await_bytes(rsr.at[d, c, part_of(h)], rsrs.at[d, h, c])
            part[c, part_of(h)] = (part[c, part_of(h)].astype(F32) + rsr[d, c, part_of(h)].astype(F32)).astype(BF)
            pass_on(c, h, way)

        loop(0, jnp.where(t < 3, 2, 1), stream)

    def finish(h):
        total_h = part[g, part_of(h)].astype(F32)
        for d in range(2):
            await_bytes(rsr.at[d, g, part_of(h)], rsrs.at[d, h, g])
            total_h = total_h + rsr[d, g, part_of(h)].astype(F32)
        ys[part_of(h)] = total_h.astype(BF)
        loop(8 * h, 8 * h + 8, give_back)

    def give_back(n):
        xt = lax.rem(n + xc, 8)
        pltpu.make_async_remote_copy(
            ys.at[8 * (n // 8) + xt], ret.at[8 * (n // 8) + xc], e3s, e3r,
            device_id={"ep": rank(xt, behind(n // 8))}, device_id_type=MESH,
        ).start()

    def give_back_near(n):
        xt = lax.rem(n + xc, 8)
        to = rank(xt, lax.rem(z + 9 - n // 8, 8))
        here, there = yn.at[8 * (n // 8) + xt], rn.at[8 * (n // 8) + xc]

        @pl.when(to == me)
        def _():
            pltpu.make_async_copy(here, there, n3r).start()

        @pl.when(to != me)
        def _():
            pltpu.make_async_remote_copy(here, there, n3s, n3r, device_id={"ep": to}, device_id_type=MESH).start()

    own_rows, forward_rows = ring(gath_at, a2s, a2r)

    def start_rows(h):
        await_bytes(gath_at(g, h), e2r.at[h])
        own_rows(h)

    loop(0, PARTS, start_rows)
    dispatch_near()
    expert_columns(g)

    def step_expert(t):
        loop(0, PARTS, lambda h: forward_rows(t, h))
        loop(0, jnp.where(t < 4, 2, 1), lambda i: expert_columns(peer(t * (2 * i - 1))))

        @pl.when(t == 1)
        def _():
            gates()

        @pl.when(t == 3)
        def _():
            await_bytes(gn, n2r)
            x = jnp.concatenate([gn[:, o].reshape(192, 256) for o in range(8)], axis=1)
            acc_g[near_rows, :] = dot_nt(x, wg[...])
            acc_u[near_rows, :] = dot_nt(x, wu[...])
            activate(near_rows)

    loop(1, 5, step_expert)
    sent.append(lambda: await_bytes(gath.at[pl.ds(0, 7)], a2s))
    activate(far_rows)
    loop(0, 5, down_block)

    def near_block(c):
        lanes = pl.ds(pl.multiple_of(c * 256, 256), 256)
        yn[:, c] = dot(act[near_rows, :], wd[:, lanes]).reshape(24, 8, 256).astype(BF)

    def mix_block(k):
        c = peer(k)
        results = rn[:, c].reshape(192, 256)
        mns[c] = (dot(mix_n[0], results) + dot(mix_n[1], results)).astype(BF)

        @pl.when(k > 0)
        def _():
            pltpu.make_async_remote_copy(
                mns.at[c], mnr.at[k - 1], mxs, mxr, device_id={"grp": c}, device_id_type=MESH
            ).start()

    loop(0, 8, near_block)
    loop(0, 24, give_back_near)

    def step_sum(t):
        loop(0, PARTS, lambda h: add_on(t, PARTS - 1 - h))

        @pl.when(t == 1)
        def _():
            loop(5, 8, down_block)

    loop(1, 4, step_sum)
    await_bytes(rn, n3r)
    loop(0, NG, lambda i: mix_block(farthest(i)))
    sent.append(lambda: await_bytes(mnr, mxs))
    sent.append(lambda: await_bytes(yn.at[pl.ds(0, 23)], n3s))
    loop(0, PARTS, lambda h: finish(PARTS - 1 - h))
    sent.append(lambda: await_bytes(part.at[pl.ds(0, 7)], rss))
    sent.append(lambda: await_bytes(ys, e3s))

    await_bytes(ret, e3r)
    results = ret[...].reshape(320, 256)
    total = st[...] + dot(mix_f[0], results) + dot(mix_f[1], results) + mns[g].astype(F32)
    await_bytes(mnr, mxr)
    for k in range(NG - 1):
        total = total + mnr[k].astype(F32)
    out[...] = total.astype(BF)

    for wait in sent:
        wait()


def local(
    hidden_in, query_nope, query_rope, new_latent, latent_cache, key_absorb, value_absorb, output_proj, norm_gain,
    router_proj, expert_ids, expert_gate, expert_up, expert_down, block_table, lengths, subtree_moves,
):
    vmem = pl.BlockSpec(memory_space=pltpu.VMEM)
    anywhere = pl.BlockSpec(memory_space=pl.ANY)
    dma = pltpu.SemaphoreType.DMA
    v = pltpu.VMEM
    return pl.pallas_call(
        kernel,
        out_shape=jax.ShapeDtypeStruct((64, 256), BF),
        in_specs=[pl.BlockSpec(memory_space=pltpu.SMEM)] + [vmem] * 7 + [anywhere] * 9,
        out_specs=vmem,
        scratch_shapes=[
            v((64, 2048), BF),
            v((16, 2304), BF),
            v((2, 512, 128), BF),
            v((256, 2048), BF),
            v((64, 2048), BF),
            v((176, 2048), BF),
            v((176, 2048), BF),
            v((176, 2048), BF),
            v((4, 8, 16, 1152), BF),
            v((8, 80, 1152), BF),
            v((8, 128, 1152), BF),
            v((128, 640), BF),
            v((128, 640), BF),
            v((128, 192), BF),
            v((128, 1), F32),
            v((128, 1), F32),
            v((128, 512), F32),
            v((128, 640), F32),
            v((8, 64, 256), BF),
            v((7, 64, 256), BF),
            v((8, 128), F32),
            v((7, 8, 128), F32),
            v((8, 64, 256), BF),
            v((64, 256), F32),
            v((40, 8, 256), BF),
            v((8, 40, 8, 256), BF),
            v((24, 8, 8, 256), BF),
            v((24, 8, 8, 256), BF),
            v((512, 176), F32),
            v((512, 176), F32),
            v((512, 176), BF),
            v((8, 40, 8, 256), BF),
            v((2, 8, 40, 8, 256), BF),
            v((40, 8, 256), BF),
            v((40, 8, 256), BF),
            v((24, 8, 8, 256), BF),
            v((24, 8, 8, 256), BF),
            v((8, 64, 256), BF),
            v((7, 64, 256), BF),
            v((2, 64, 192), BF),
            v((2, 64, 320), BF),
            dma, dma((8,)),
            dma, dma((5,)), dma((3,)), dma((3,)), dma, dma((5, 8)),
            dma, dma, dma, dma, dma, dma,
            dma, dma((5,)), dma, dma, dma, dma((5, 8)),
            dma, dma((2, 5, 8)),
            dma, dma, dma, dma, dma, dma,
        ],
        compiler_params=pltpu.CompilerParams(
            collective_id=0, has_side_effects=True, vmem_limit_bytes=56 * 1024 * 1024
        ),
        name="layer",
    )(
        lengths, query_nope, query_rope, key_absorb, norm_gain, expert_ids.T, block_table, subtree_moves[0].T,
        hidden_in, new_latent, value_absorb, output_proj, router_proj.T,
        latent_cache, expert_gate[0].T, expert_up[0].T, expert_down,
    )


def solution(mesh):
    in_specs = (
        P("ep", None), P("ep", "grp"), P("ep", "grp"), P("ep", None), P("ep", None),
        P("grp", None, None), P("grp", None, None), P("grp", None), P(), P(), P("ep", None),
        P("ep", None, "grp"), P("ep", None, "grp"), P("ep", "grp", None), P("ep", None), P("ep"),
        P("ep", None, None),
    )
    return jax.shard_map(local, mesh=mesh, in_specs=in_specs, out_specs=P("ep", "grp"), check_vma=False)
```
